128 devices in a mesh: emit: 8 (over x_hi, z), elem: 16 (over y, x_lo, core).
Axes of the slice: x: 4 (x_hi: 2, x_lo: 2; x = x_hi * 2 + x_lo), y: 4, z: 4, core: 2. Of those that a mesh axis runs over, the one named last changes fastest.
Arguments:
- traces: float32 [256, 1024, 1024], P('emit', 'elem'), may hold values from -6 to 6
- codes: float32 [4, 2, 128], replicated, may hold values from -0.5 to 0.5
- code_of: int32 [256], replicated, may hold values from 0 to 3
- order: int32 [256], replicated, may hold values from 0 to 255, each once
- steer: float32 [256, 1024, 256], P(None, 'elem'), may hold values from -0.1875 to 0.1875
Outputs:
- beams: float32 [256, 256, 256], P('elem', 'emit')
The draws below stay inside these ranges and needn't reach their ends.
Inputs may be any that keep to these rules, and one draw needn't show every extreme that they name: `order`: each value 0 to 255 appears exactly once.
All inputs are finite; a program needn't handle non-finite values.
Results may differ from the reference program's by a relative error of at most 0.000071.
Values sent between devices are 32-bit elements; how exact they have to be, the bound alone decides.
A program may use at most 192 MiB of HBM per device.

```python
import jax
import jax.numpy as jnp
from jax import lax

E = 256
M = 1024
S = 1024
TAPS = 128
NB = 256
L = 128
NCODE = 4


def place_ends(result, own_key, low, top_value):
    shape = result.shape
    index_at = [jax.random.randint(jax.random.fold_in(own_key, axis), (), 0, shape[axis]) for axis in range(len(shape))]
    result = result.at[tuple(index_at)].set(low)
    longest = shape.index(max(shape))
    index_at[longest] = (index_at[longest] + 1) % shape[longest]
    return result.at[tuple(index_at)].set(top_value)


def raised(drawn, own_key, source, target, shards_of, factor):
    def block_of(dim):
        return (jnp.arange(drawn.shape[dim]) // (drawn.shape[dim] // shards_of)).reshape((-1,) + (1,) * (drawn.ndim - 1 - dim))

    first = jax.random.permutation(own_key, shards_of)[block_of(target)]
    second = (block_of(target) + shards_of // 2) % shards_of
    return jnp.where((block_of(source) == first) | (block_of(source) == second), factor * drawn, drawn)


def level_of(key, extent, pieces, low, high):
    level, own = 1.0, jax.random.fold_in(key, 6)
    for dim, shards_of in pieces:
        steps = jnp.exp(jax.random.uniform(jax.random.fold_in(own, dim), (shards_of,), jnp.float32, low / len(pieces), high / len(pieces)))
        level = level * jnp.repeat(steps, extent[dim] // shards_of).reshape([-1 if axis == dim else 1 for axis in range(len(extent))])
    return level


def centred(rng, shape, deviation, bound, pieces=(), held_as=jnp.bfloat16):
    entries = deviation * jax.random.normal(rng, shape, jnp.float32)
    if pieces:
        entries = entries * level_of(rng, shape, pieces, -0.22, 0.18)
    return jnp.clip(entries, -bound, bound).astype(held_as)


def noise_with(stream_key, extent, scale, bound, pieces, heavy, kind=jnp.bfloat16):
    values = scale * jax.random.normal(stream_key, extent, jnp.float32)
    if pieces:
        values = values * level_of(stream_key, extent, pieces, -0.22, 0.18)
    return jnp.clip(raised(values, jax.random.fold_in(stream_key, 3), *heavy), -bound, bound).astype(kind)


def setup_inputs(seed: int = 0) -> dict:
    key_of = jax.random.split(jax.random.key(seed), 6)
    return {
        "traces": centred(key_of[0], (E, M, S), 1.0, 6.0, ((0, 8), (1, 16)), jnp.float32),
        "codes": centred(key_of[1], (NCODE, 2, TAPS), TAPS ** -0.5, 0.5, (), jnp.float32),
        "code_of": place_ends(jax.random.randint(key_of[2], (E,), 0, NCODE), jax.random.fold_in(key_of[2], 1), 0, NCODE - 1).astype(jnp.int32),
        "order": jax.random.permutation(key_of[3], E).astype(jnp.int32),
        "steer": noise_with(key_of[4], (NB, M, 2 * L), (2 * M) ** -0.5, 0.1875, ((1, 16),), (1, 0, 16, 2.0), jnp.float32),
    }


def toeplitz_table(codes):
    taps = codes.shape[2]
    rows = jnp.arange(2 * taps, dtype=jnp.int32)[:, None]
    cols = jnp.arange(taps, dtype=jnp.int32)[None, :]
    offset = rows - cols
    inside = (offset >= 0) & (offset < taps)
    clipped = jnp.clip(offset, 0, taps - 1)
    in_phase = jnp.where(inside[None], codes[:, 0, :][:, clipped], 0.0)
    quadrature = jnp.where(inside[None], codes[:, 1, :][:, clipped], 0.0)
    return jnp.concatenate([in_phase, quadrature], axis=2).astype(jnp.float32)

def hadamard_signs(order, columns, emissions):
    parity = jnp.zeros((order.shape[0], columns.shape[0]), jnp.int32)
    for bit in range(emissions.bit_length()):
        parity = parity + (order[:, None] >> bit & columns[None, :] >> bit & 1)
    signs = (1 - 2 * (parity % 2)).astype(jnp.float32)
    return signs / jnp.sqrt(jnp.float32(emissions))

def reference(traces, codes, code_of, order, steer):
    table = toeplitz_table(codes)
    nblock = S // TAPS
    freqs = jnp.mod(jnp.arange(NB, dtype=jnp.int32) - NB // 2, S).astype(jnp.int32)

    def one_emission(args):
        trace, code_index = args
        padded = jnp.concatenate([trace, jnp.zeros((M, TAPS), trace.dtype)], axis=1).reshape(M, nblock + 1, TAPS)
        windows = jnp.concatenate([padded[:, :-1], padded[:, 1:]], axis=2)
        picked = table[code_index]
        corr = jnp.einsum('mnj,jd->mnd', windows, picked, precision=lax.Precision.HIGHEST)
        corr_i = corr[:, :, :TAPS].reshape(M, S)
        corr_q = corr[:, :, TAPS:].reshape(M, S)
        spectrum = jnp.fft.fft(corr_i + 1j * corr_q, axis=1)[:, freqs] / jnp.sqrt(jnp.float32(S))
        return jnp.concatenate([jnp.real(spectrum), jnp.imag(spectrum)], axis=1).astype(traces.dtype)
    spectra = lax.map(one_emission, (traces, code_of))
    hadamard = hadamard_signs(order, jnp.arange(E, dtype=jnp.int32), E)
    decoded = jnp.dot(hadamard.T, spectra.reshape(E, M * 2 * NB), precision=lax.Precision.HIGHEST).reshape(E, M, 2 * NB)
    real_part = decoded[:, :, :NB]
    imag_part = decoded[:, :, NB:]
    first = jnp.einsum('kmb,bml->bkl', real_part, steer, precision=lax.Precision.HIGHEST)
    second = jnp.einsum('kmb,bml->bkl', imag_part, steer, precision=lax.Precision.HIGHEST)
    return jnp.concatenate([first[..., :L] - second[..., L:], first[..., L:] + second[..., :L]], axis=2)
```

```python
import functools
import numpy as np
import jax
import jax.numpy as jnp
from jax import lax
from jax.experimental import pallas as pl
from jax.experimental.pallas import tpu as pltpu

from jax.sharding import PartitionSpec as P

HIGH = lax.Precision.HIGH
NT = (((1,), (1,)), ((), ()))


def dft_tables(samples, taps, half):
    t = np.arange(taps, samples)
    pos = np.arange(half)
    cosine = np.cos(2 * np.pi * (pos[:, None] * t[None] % samples) / samples)
    sine = np.sin(2 * np.pi * (pos[:, None] * t[None] % samples) / samples)
    top = 2 * np.pi * (half * t % samples) / samples
    sine[0] = np.cos(top)
    extra = np.zeros((8, t.size))
    extra[0] = np.sin(top)
    body = np.concatenate([cosine, sine, extra], 0).astype(np.float32)
    freq = np.concatenate([pos, np.where(pos == 0, -half, -pos)])
    u = np.arange(taps)
    angle = 2 * np.pi * (freq[:, None] * u[None] % samples) / samples
    head = np.stack([np.cos(angle), np.sin(angle)]).astype(np.float32)
    tri = (u[:, None] <= u[None, :]).astype(np.float32)
    return body, head, tri


def spectra_kernel(scale, code_ref, codes_ref, head_ref, tri_ref, body_ref, x_ref, out_ref, gain_ref, tab_ref):
    step = pl.program_id(0)
    ncode, _, taps = codes_ref.shape
    eblk, mdev, samples = x_ref.shape
    half = out_ref.shape[1]
    nrow = 2 * half

    @pl.when(step == 0)
    def _():
        cosine, sine = head_ref[0], head_ref[1]
        for c in range(ncode):
            ci = codes_ref[c, 0:1, :] * scale
            cq = codes_ref[c, 1:2, :] * scale
            a_re = ci * cosine - cq * sine
            a_im = ci * sine + cq * cosine
            p_re = jnp.dot(a_re, tri_ref[...], precision=lax.Precision.HIGHEST, preferred_element_type=jnp.float32)
            p_im = jnp.dot(a_im, tri_ref[...], precision=lax.Precision.HIGHEST, preferred_element_type=jnp.float32)
            lanes = slice(c * taps, (c + 1) * taps)
            gain_ref[0:nrow, lanes] = cosine * p_re + sine * p_im
            gain_ref[nrow:, lanes] = cosine * p_im - sine * p_re
            tab_ref[c, 0:nrow] = jnp.broadcast_to(p_re[:, taps - 1:], (nrow, 128))
            tab_ref[c, nrow:] = jnp.broadcast_to(p_im[:, taps - 1:], (nrow, 128))

    x = x_ref[...].reshape(eblk * mdev, samples)
    spec = lax.dot_general(body_ref[...], x[:, taps:], NT, precision=HIGH, preferred_element_type=jnp.float32)
    codes = [code_ref[step * eblk + e] for e in range(eblk)]
    masked = jnp.concatenate(
        [
            jnp.concatenate(
                [x_ref[e, :, 0:taps] * (codes[e] == c).astype(jnp.float32) for e in range(eblk)], axis=0
            )
            for c in range(ncode)
        ],
        axis=1,
    )
    corr = lax.dot_general(gain_ref[...], masked, NT, precision=HIGH, preferred_element_type=jnp.float32)
    first = lax.broadcasted_iota(jnp.int32, (half, 128), 0) == 0
    left = lax.broadcasted_iota(jnp.int32, (half, 128), 1) < mdev
    for sign in range(2):
        rows = slice(sign * half, (sign + 1) * half)
        irows = slice(nrow + sign * half, nrow + (sign + 1) * half)
        planes = []
        for q in range(eblk // 2):
            lanes = slice(q * 128, (q + 1) * 128)
            xc, xs = spec[0:half, lanes], spec[half:nrow, lanes]
            cr = jnp.where(left, tab_ref[codes[2 * q], rows], tab_ref[codes[2 * q + 1], rows])
            ci = jnp.where(left, tab_ref[codes[2 * q], irows], tab_ref[codes[2 * q + 1], irows])
            if sign == 0:
                xs = jnp.where(first, 0.0, -xs)
            else:
                xc = jnp.where(first, xs, xc)
                xs = jnp.where(first, spec[nrow:nrow + 1, lanes], xs)
            re = xc * cr - xs * ci + corr[rows, lanes]
            im = xc * ci + xs * cr + corr[irows, lanes]
            planes.append(jnp.where(left, re, pltpu.roll(im, 64, 1)))
            planes.append(jnp.where(left, pltpu.roll(re, 64, 1), im))
        out_ref[sign] = jnp.swapaxes(jnp.stack(planes, 0), 0, 1)


def spectra(traces, codes, own_codes, nb=256):
    edev, mdev, samples = traces.shape
    ncode, _, taps = codes.shape
    half = nb // 2
    body, head, tri = dft_tables(samples, taps, half)
    eblk = 8
    full = lambda s: pl.BlockSpec(s, lambda i: (0,) * len(s))
    return pl.pallas_call(
        functools.partial(spectra_kernel, float(samples) ** -0.5),
        grid=(edev // eblk,),
        in_specs=[
            pl.BlockSpec(memory_space=pltpu.SMEM),
            full(codes.shape), full(head.shape), full(tri.shape), full(body.shape),
            pl.BlockSpec((eblk, mdev, samples), lambda i: (i, 0, 0)),
        ],
        out_specs=pl.BlockSpec((2, half, eblk, 2 * mdev), lambda i: (0, 0, i, 0)),
        out_shape=jax.ShapeDtypeStruct((2, half, edev, 2 * mdev), jnp.float32),
        scratch_shapes=[
            pltpu.VMEM((4 * half, ncode * taps), jnp.float32),
            pltpu.VMEM((ncode, 4 * half, 128), jnp.float32),
        ],
        compiler_params=pltpu.CompilerParams(vmem_limit_bytes=56 << 20),
        name="spectra",
    )(own_codes, codes, head, tri, body, traces)


def steer_kernel(d_ref, s_ref, out_ref):
    step = pl.program_id(0)
    blk, mdev, width = s_ref.shape
    half = d_ref.shape[1]
    lines = width // 2

    def one(k, carry):
        b = step * blk + k
        sign = 1 - b // half
        row = (b - half) * (1 - 2 * sign)
        row = lax.rem(row, half)
        d = d_ref[sign, row]
        s = s_ref[k]
        w = jnp.concatenate([s, jnp.concatenate([-s[:, lines:], s[:, :lines]], axis=1)], axis=0)
        out_ref[k] = jnp.dot(d, w, precision=HIGH, preferred_element_type=jnp.float32)
        return carry

    lax.fori_loop(0, blk, one, 0, unroll=True)


def steered(decoded, steer):
    bins, mdev, width = steer.shape
    edev = decoded.shape[2]
    blk = 16
    return pl.pallas_call(
        steer_kernel,
        grid=(bins // blk,),
        in_specs=[
            pl.BlockSpec(decoded.shape, lambda i: (0, 0, 0, 0)),
            pl.BlockSpec((blk, mdev, width), lambda i: (i, 0, 0)),
        ],
        out_specs=pl.BlockSpec((blk, edev, width), lambda i: (i, 0, 0)),
        out_shape=jax.ShapeDtypeStruct((bins, edev, width), jnp.float32),
        compiler_params=pltpu.CompilerParams(vmem_limit_bytes=56 << 20),
        name="steer",
    )(decoded, steer)


def hadamard_signs(order, columns):
    both = order[:, None] & columns[None, :]
    parity = lax.population_count(both) & 1
    return (1 - 2 * parity).astype(jnp.float32) / jnp.sqrt(jnp.float32(order.shape[0]))


def per_device(traces, codes, code_of, order, steer):
    edev = traces.shape[0]
    emissions = order.shape[0]
    first = lax.axis_index("emit") * edev
    own_codes = lax.dynamic_slice_in_dim(code_of, first, edev)
    spec = spectra(traces, codes, own_codes, steer.shape[0])
    part = steered(spec, steer)
    summed = lax.psum_scatter(part, "elem", scatter_dimension=0, tiled=True)
    gathered = lax.all_to_all(summed, "emit", 0, 1, tiled=True)
    hadamard = hadamard_signs(order, jnp.arange(emissions, dtype=jnp.int32))
    decoded = jnp.einsum("ek,bel->bkl", hadamard, gathered, precision=lax.Precision.HIGHEST)
    return lax.all_to_all(decoded, "emit", 1, 0, tiled=True)


def solution(mesh):
    placed = (P("emit", "elem", None), P(), P(), P(), P(None, "elem", None))
    return jax.shard_map(
        per_device, mesh=mesh, in_specs=placed, out_specs=P("elem", "emit", None), check_vma=False
    )
```

```python
import functools
import numpy as np
import jax
import jax.numpy as jnp
from jax import lax
from jax.experimental import pallas as pl
from jax.experimental.pallas import tpu as pltpu

from jax.sharding import PartitionSpec as P

HIGH = lax.Precision.HIGH
NT = (((1,), (1,)), ((), ()))


def dft_tables(samples, taps, half):
    t = np.arange(taps, samples)
    pos = np.arange(half)
    cosine = np.cos(2 * np.pi * (pos[:, None] * t[None] % samples) / samples)
    sine = np.sin(2 * np.pi * (pos[:, None] * t[None] % samples) / samples)
    top = 2 * np.pi * (half * t % samples) / samples
    sine[0] = np.cos(top)
    extra = np.zeros((8, t.size))
    extra[0] = np.sin(top)
    body = np.concatenate([cosine, sine, extra], 0).astype(np.float32)
    freq = np.concatenate([pos, np.where(pos == 0, -half, -pos)])
    u = np.arange(taps)
    angle = 2 * np.pi * (freq[:, None] * u[None] % samples) / samples
    head = np.stack([np.cos(angle), np.sin(angle)]).astype(np.float32)
    tri = (u[:, None] <= u[None, :]).astype(np.float32)
    return body, head, tri


def spectra_kernel(scale, code_ref, codes_ref, head_ref, tri_ref, body_ref, x_ref, out_ref, gain_ref, tab_ref):
    step = pl.program_id(0)
    ncode, _, taps = codes_ref.shape
    eblk, mdev, samples = x_ref.shape
    half = out_ref.shape[1]
    nrow = 2 * half

    @pl.when(step == 0)
    def _():
        cosine, sine = head_ref[0], head_ref[1]
        for c in range(ncode):
            ci = codes_ref[c, 0:1, :] * scale
            cq = codes_ref[c, 1:2, :] * scale
            a_re = ci * cosine - cq * sine
            a_im = ci * sine + cq * cosine
            p_re = jnp.dot(a_re, tri_ref[...], precision=lax.Precision.HIGHEST, preferred_element_type=jnp.float32)
            p_im = jnp.dot(a_im, tri_ref[...], precision=lax.Precision.HIGHEST, preferred_element_type=jnp.float32)
            lanes = slice(c * taps, (c + 1) * taps)
            gain_ref[0:nrow, lanes] = cosine * p_re + sine * p_im
            gain_ref[nrow:, lanes] = cosine * p_im - sine * p_re
            tab_ref[c, 0:nrow] = jnp.broadcast_to(p_re[:, taps - 1:], (nrow, 128))
            tab_ref[c, nrow:] = jnp.broadcast_to(p_im[:, taps - 1:], (nrow, 128))

    x = x_ref[...].reshape(eblk * mdev, samples)
    spec = lax.dot_general(body_ref[...], x[:, taps:], NT, precision=HIGH, preferred_element_type=jnp.float32)
    codes = [code_ref[step * eblk + e] for e in range(eblk)]
    masked = jnp.concatenate(
        [
            jnp.concatenate(
                [x_ref[e, :, 0:taps] * (codes[e] == c).astype(jnp.float32) for e in range(eblk)], axis=0
            )
            for c in range(ncode)
        ],
        axis=1,
    )
    corr = lax.dot_general(gain_ref[...], masked, NT, precision=HIGH, preferred_element_type=jnp.float32)
    first = lax.broadcasted_iota(jnp.int32, (half, 128), 0) == 0
    left = lax.broadcasted_iota(jnp.int32, (half, 128), 1) < mdev
    for sign in range(2):
        rows = slice(sign * half, (sign + 1) * half)
        irows = slice(nrow + sign * half, nrow + (sign + 1) * half)
        planes = []
        for q in range(eblk // 2):
            lanes = slice(q * 128, (q + 1) * 128)
            xc, xs = spec[0:half, lanes], spec[half:nrow, lanes]
            cr = jnp.where(left, tab_ref[codes[2 * q], rows], tab_ref[codes[2 * q + 1], rows])
            ci = jnp.where(left, tab_ref[codes[2 * q], irows], tab_ref[codes[2 * q + 1], irows])
            if sign == 0:
                xs = jnp.where(first, 0.0, -xs)
            else:
                xc = jnp.where(first, xs, xc)
                xs = jnp.where(first, spec[nrow:nrow + 1, lanes], xs)
            re = xc * cr - xs * ci + corr[rows, lanes]
            im = xc * ci + xs * cr + corr[irows, lanes]
            planes.append(jnp.where(left, re, pltpu.roll(im, 64, 1)))
            planes.append(jnp.where(left, pltpu.roll(re, 64, 1), im))
        out_ref[sign] = jnp.swapaxes(jnp.stack(planes, 0), 0, 1)


def spectra(traces, codes, own_codes, nb=256):
    edev, mdev, samples = traces.shape
    ncode, _, taps = codes.shape
    half = nb // 2
    body, head, tri = dft_tables(samples, taps, half)
    eblk = 8
    full = lambda s: pl.BlockSpec(s, lambda i: (0,) * len(s))
    return pl.pallas_call(
        functools.partial(spectra_kernel, float(samples) ** -0.5),
        grid=(edev // eblk,),
        in_specs=[
            pl.BlockSpec(memory_space=pltpu.SMEM),
            full(codes.shape), full(head.shape), full(tri.shape), full(body.shape),
            pl.BlockSpec((eblk, mdev, samples), lambda i: (i, 0, 0)),
        ],
        out_specs=pl.BlockSpec((2, half, eblk, 2 * mdev), lambda i: (0, 0, i, 0)),
        out_shape=jax.ShapeDtypeStruct((2, half, edev, 2 * mdev), jnp.float32),
        scratch_shapes=[
            pltpu.VMEM((4 * half, ncode * taps), jnp.float32),
            pltpu.VMEM((ncode, 4 * half, 128), jnp.float32),
        ],
        compiler_params=pltpu.CompilerParams(vmem_limit_bytes=56 << 20),
        name="spectra",
    )(own_codes, codes, head, tri, body, traces)


MESH = pl.DeviceIdType.MESH
ROUNDS = 16
SLOT_Y = (2, 1, 2, 3, 1, 3, 0, 0)
SLOT_X = (0, 1, 1, 0, 0, 1, 0, 1)


def beam_kernel(
    order_ref, d_ref, steer_ref, out_ref,
    wbuf, sendc, recvc, acc, recv1, recv2, fwd, totx, recvx, fin, gath, dec, had,
    wsem, csem, crsem, ysem, yrsem, y2sem, y2rsem, xsem, xrsem, asem, arsem, osem, orsem,
):
    i, j = lax.axis_index("emit"), lax.axis_index("elem")
    y, x, c = j // 4, j // 2 % 2, j % 2
    nemit = 8
    half, edev = d_ref.shape[1], d_ref.shape[2]
    lines = steer_ref.shape[3] // 2

    def at(yy, xx, cc):
        return (i, (yy * 2 + xx) * 2 + cc)

    other_core = at(y, x, 1 - c)
    up, down = at((y + 1) % 4, x, c), at((y + 3) % 4, x, c)
    other_x = at(y, 1 - x, c)

    def emit_peer(q):
        return ((i + q) % nemit, j)

    def bin_of(t):
        return (i + t) % nemit * 2 + t // nemit

    def remote(src, dst, ssem, rsem, device):
        return pltpu.make_async_remote_copy(
            src_ref=src, dst_ref=dst, send_sem=ssem, recv_sem=rsem, device_id=device, device_id_type=MESH
        )

    def load(t):
        return pltpu.make_async_copy(steer_ref.at[:, bin_of(t)], wbuf.at[t % 4], wsem.at[t % 4])

    def core_copy(t):
        return remote(sendc.at[t], recvc.at[t], csem.at[t], crsem.at[t], other_core)

    def y1_copy(t, d):
        return remote(acc.at[t, pl.ds(2 * d, 2)], recv1.at[t, d], ysem.at[t, d], yrsem.at[t, d], up if d == 0 else down)

    def y2_copy(t, d):
        return remote(fwd.at[t, d], recv2.at[t, d], y2sem.at[t, d], y2rsem.at[t, d], up if d == 0 else down)

    def x_copy(t):
        return remote(totx.at[t], recvx.at[t], xsem.at[t], xrsem.at[t], other_x)

    def a_copy(t):
        q = t % nemit
        return remote(
            fin.at[t], gath.at[t // nemit, pl.ds(pl.multiple_of(i * edev, edev), edev)], asem.at[t], arsem.at[t], emit_peer(q)
        )

    def o_copy(s, q):
        k = (i + q) % nemit
        return remote(
            dec.at[s, pl.ds(pl.multiple_of(k * edev, edev), edev)], out_ref.at[2 * i + s], osem.at[s, q], orsem.at[s, q], emit_peer(q)
        )

    load(0).start()
    load(1).start()
    barrier = pltpu.get_barrier_semaphore()
    peers = [other_core, up, down, other_x] + [emit_peer(q) for q in range(1, nemit)]
    for peer in peers:
        pl.semaphore_signal(barrier, inc=1, device_id=peer, device_id_type=MESH)
    both = order_ref[...] & lax.broadcasted_iota(jnp.int32, had.shape, 0)
    for shift in (4, 2, 1):
        both = both ^ (both >> shift)
    had[...] = ((1 - 2 * (both & 1)).astype(jnp.float32) * (had.shape[0] ** -0.5)).astype(jnp.bfloat16)
    pl.semaphore_wait(barrier, len(peers))

    def product(t, slot, core):
        jj = ((y + SLOT_Y[slot]) % 4 * 2 + SLOT_X[slot]) * 2 + core
        b = jj * 16 + bin_of(t)
        sign = 1 - b // half
        row = (b - half) * (1 - 2 * sign) % half
        s = wbuf[t % 4, jj]
        w = jnp.concatenate([s, jnp.concatenate([-s[:, lines:], s[:, :lines]], axis=1)], axis=0)
        return jnp.dot(d_ref[sign, row], w, precision=HIGH, preferred_element_type=jnp.float32)

    def decode(s):
        for q in range(1, nemit):
            a_copy(s * nemit + q).wait_recv()
        g = gath[s]
        hi = g.astype(jnp.bfloat16)
        lo = (g - hi.astype(jnp.float32)).astype(jnp.bfloat16)
        h = had[...]
        dec[s] = jnp.dot(h, hi, preferred_element_type=jnp.float32) + jnp.dot(h, lo, preferred_element_type=jnp.float32)
        for q in range(1, nemit):
            o_copy(s, q).start()
        out_ref[2 * i + s] = dec[s, pl.ds(pl.multiple_of(i * edev, edev), edev)]

    def body(t, carry):
        @pl.when(t + 2 < ROUNDS)
        def _():
            load(t + 2).start()

        @pl.when(t < ROUNDS)
        def _():
            load(t).wait()
            for slot in range(8):
                sendc[t, slot] = product(t, slot, 1 - c)
            core_copy(t).start()

        @pl.when((t >= 1) & (t < ROUNDS + 1))
        def _():
            u = t - 1
            core_copy(u).wait_recv()
            for slot in range(8):
                acc[u, slot] = product(u, slot, c) + recvc[u, slot]
                if slot == 1:
                    y1_copy(u, 0).start()
                if slot == 3:
                    y1_copy(u, 1).start()

        @pl.when((t >= 2) & (t < ROUNDS + 2))
        def _():
            u = t - 2
            for d in range(2):
                y1_copy(u, d).wait_recv()
                fwd[u, d] = acc[u, 4 + d] + recv1[u, d, 0]
                y2_copy(u, d).start()

        @pl.when((t >= 3) & (t < ROUNDS + 3))
        def _():
            u = t - 3
            for d in range(2):
                y2_copy(u, d).wait_recv()
            tot0 = acc[u, 6] + recv2[u, 0] + recv1[u, 1, 1]
            tot1 = acc[u, 7] + recv2[u, 1] + recv1[u, 0, 1]
            mine = (x == 0).astype(jnp.float32)
            totx[u] = tot1 * mine + tot0 * (1.0 - mine)
            fin[u] = tot0 * mine + tot1 * (1.0 - mine)
            x_copy(u).start()

        @pl.when((t >= 4) & (t < ROUNDS + 4))
        def _():
            u = t - 4
            x_copy(u).wait_recv()
            fin[u] = fin[u] + recvx[u]

            @pl.when(u % nemit == 0)
            def _():
                gath[u // nemit, pl.ds(pl.multiple_of(i * edev, edev), edev)] = fin[u]

            @pl.when(u % nemit != 0)
            def _():
                a_copy(u).start()

        @pl.when(t == nemit + 5)
        def _():
            decode(0)

        return carry

    lax.fori_loop(0, ROUNDS + 4, body, 0)
    decode(1)

    def drain(t, carry):
        core_copy(t).wait_send()
        for d in range(2):
            y1_copy(t, d).wait_send()
            y2_copy(t, d).wait_send()
        x_copy(t).wait_send()

        @pl.when(t % nemit != 0)
        def _():
            a_copy(t).wait_send()

        return carry

    lax.fori_loop(0, ROUNDS, drain, 0)
    for s in range(2):
        for q in range(1, nemit):
            o_copy(s, q).wait()


def beams(order, spec, steer):
    bins, mdev, width = steer.shape
    edev = spec.shape[2]
    emissions = order.shape[0]
    block = (edev, width)
    f32 = jnp.float32
    dma = pltpu.SemaphoreType.DMA
    vmem = pl.BlockSpec(memory_space=pltpu.VMEM)
    return pl.pallas_call(
        beam_kernel,
        in_specs=[vmem, vmem, pl.BlockSpec(memory_space=pl.ANY)],
        out_specs=vmem,
        out_shape=jax.ShapeDtypeStruct((16, edev, width), f32),
        scratch_shapes=[
            pltpu.VMEM((4, 16, mdev, width), f32),
            pltpu.VMEM((ROUNDS, 8) + block, f32),
            pltpu.VMEM((ROUNDS, 8) + block, f32),
            pltpu.VMEM((ROUNDS, 8) + block, f32),
            pltpu.VMEM((ROUNDS, 2, 2) + block, f32),
            pltpu.VMEM((ROUNDS, 2) + block, f32),
            pltpu.VMEM((ROUNDS, 2) + block, f32),
            pltpu.VMEM((ROUNDS,) + block, f32),
            pltpu.VMEM((ROUNDS,) + block, f32),
            pltpu.VMEM((ROUNDS,) + block, f32),
            pltpu.VMEM((2, emissions, width), f32),
            pltpu.VMEM((2, emissions, width), f32),
            pltpu.VMEM((emissions, emissions), jnp.bfloat16),
            dma((4,)), dma((ROUNDS,)), dma((ROUNDS,)), dma((ROUNDS, 2)), dma((ROUNDS, 2)), dma((ROUNDS, 2)), dma((ROUNDS, 2)),
            dma((ROUNDS,)), dma((ROUNDS,)), dma((ROUNDS,)), dma((ROUNDS,)), dma((2, 8)), dma((2, 8)),
        ],
        compiler_params=pltpu.CompilerParams(collective_id=0, has_side_effects=True, vmem_limit_bytes=60 << 20),
        name="beams",
    )(order.reshape(1, emissions), spec, steer.reshape(16, bins // 16, mdev, width))


def per_device(traces, codes, code_of, order, steer):
    edev = traces.shape[0]
    first = lax.axis_index("emit") * edev
    own_codes = lax.dynamic_slice_in_dim(code_of, first, edev)
    spec = spectra(traces, codes, own_codes, steer.shape[0])
    return beams(order, spec, steer)


def solution(mesh):
    placed = (P("emit", "elem", None), P(), P(), P(), P(None, "elem", None))
    return jax.shard_map(
        per_device, mesh=mesh, in_specs=placed, out_specs=P("elem", "emit", None), check_vma=False
    )
```

```python
import functools

import numpy as np
import jax
import jax.numpy as jnp
from jax import lax
from jax.experimental import pallas as pl
from jax.experimental.pallas import tpu as pltpu
from jax.sharding import PartitionSpec as P

HIGH = lax.Precision.HIGH
NT = (((1,), (1,)), ((), ()))
MESH = pl.DeviceIdType.MESH
ROUNDS = 16
LAG_B, LAG_C, LAG_D, LAG_E = 1, 3, 5, 7
SLOTS = 8
SLOT_Y = (2, 1, 2, 3, 1, 3, 0, 0)
SLOT_X = (0, 1, 1, 0, 0, 1, 0, 1)
RESIDUES = ((0, 8, 1, 15, 2, 14, 3, 13), (4, 12, 5, 11, 6, 10, 7, 9))
EBLK = 8
QUART = 64


def dft_tables(samples, taps):
    t = np.arange(taps, samples)
    u = np.arange(taps)
    bodies, heads = [], []
    for g in range(2):
        freq = (16 * np.arange(8)[:, None] + np.array(RESIDUES[g])[None, :]).reshape(-1)
        angle = 2 * np.pi * (freq[:, None] * t[None] % samples) / samples
        cosine, sine, extra = np.cos(angle), np.sin(angle), np.zeros((8, t.size))
        if g == 0:
            top = 2 * np.pi * (128 * t % samples) / samples
            sine[0], extra[0] = np.cos(top), np.sin(top)
        bodies.append(np.concatenate([cosine, sine, extra], 0))
        both = np.concatenate([freq, np.where(freq == 0, -128, -freq)])
        angle = 2 * np.pi * (both[:, None] * u[None] % samples) / samples
        heads.append(np.stack([np.cos(angle), np.sin(angle)]))
    tri = (u[:, None] <= u[None, :]).astype(np.float32)
    return np.stack(bodies).astype(np.float32), np.stack(heads).astype(np.float32), tri


def fill_tables(g, codes_ref, head_ref, tri_ref, gain_ref, tab_ref, scale):
    ncode, _, taps = codes_ref.shape
    cosine, sine = head_ref[g, 0], head_ref[g, 1]
    nrow = 2 * QUART
    for c in range(ncode):
        ci = codes_ref[c, 0:1, :] * scale
        cq = codes_ref[c, 1:2, :] * scale
        a_re = ci * cosine - cq * sine
        a_im = ci * sine + cq * cosine
        p_re = jnp.dot(a_re, tri_ref[...], precision=HIGH, preferred_element_type=jnp.float32)
        p_im = jnp.dot(a_im, tri_ref[...], precision=HIGH, preferred_element_type=jnp.float32)
        lanes = slice(c * taps, (c + 1) * taps)
        gain_ref[g, 0:nrow, lanes] = cosine * p_re + sine * p_im
        gain_ref[g, nrow:, lanes] = cosine * p_im - sine * p_re
        tab_ref[g, c, 0:nrow] = jnp.broadcast_to(p_re[:, taps - 1:], (nrow, 128))
        tab_ref[g, c, nrow:] = jnp.broadcast_to(p_im[:, taps - 1:], (nrow, 128))


def transform(g, blk, first_code, code_ref, x_ref, body_ref, gain_ref, tab_ref, spec_ref):
    _, mdev, samples = x_ref.shape
    ncode, taps = tab_ref.shape[1], gain_ref.shape[2] // tab_ref.shape[1]
    nrow = 2 * QUART
    start = pl.multiple_of(blk * EBLK, EBLK)
    x = x_ref[pl.ds(start, EBLK)].reshape(EBLK * mdev, samples)
    spec = lax.dot_general(body_ref[g], x[:, taps:], NT, precision=HIGH, preferred_element_type=jnp.float32)
    codes = [code_ref[first_code + start + e] for e in range(EBLK)]
    masked = jnp.concatenate(
        [
            jnp.concatenate(
                [x_ref[start + e, :, 0:taps] * (codes[e] == c).astype(jnp.float32) for e in range(EBLK)], axis=0
            )
            for c in range(ncode)
        ],
        axis=1,
    )
    corr = lax.dot_general(gain_ref[g], masked, NT, precision=HIGH, preferred_element_type=jnp.float32)
    first = lax.broadcasted_iota(jnp.int32, (QUART, 128), 0) == 0
    left = lax.broadcasted_iota(jnp.int32, (QUART, 128), 1) < mdev
    for sign in range(2):
        rows = slice(sign * QUART, (sign + 1) * QUART)
        irows = slice(nrow + sign * QUART, nrow + (sign + 1) * QUART)
        planes = []
        for q in range(EBLK // 2):
            lanes = slice(q * 128, (q + 1) * 128)
            xc, xs = spec[0:QUART, lanes], spec[QUART:nrow, lanes]
            cr = jnp.where(left, tab_ref[g, codes[2 * q], rows], tab_ref[g, codes[2 * q + 1], rows])
            ci = jnp.where(left, tab_ref[g, codes[2 * q], irows], tab_ref[g, codes[2 * q + 1], irows])
            if sign == 0:
                xs = jnp.where(first, 0.0, -xs) if g == 0 else -xs
            elif g == 0:
                xc = jnp.where(first, xs, xc)
                xs = jnp.where(first, spec[nrow:nrow + 1, lanes], xs)
            re = xc * cr - xs * ci + corr[rows, lanes]
            im = xc * ci + xs * cr + corr[irows, lanes]
            planes.append(jnp.where(left, re, pltpu.roll(im, 64, 1)))
            planes.append(jnp.where(left, pltpu.roll(re, 64, 1), im))
        spec_ref[g, sign, :, pl.ds(start, EBLK), :] = jnp.swapaxes(jnp.stack(planes, 0), 0, 1)


def beam_kernel(
    code_ref, codes_hbm, head_hbm, tri_hbm, body_hbm, order_hbm, traces_ref, steer_ref, out_ref,
    codes_ref, head_ref, tri_ref, body_ref, order_ref, xbuf, gain, tab, spec, wbuf, sendc, recvc, acc, recv1, recv2, fwd, totx, recvx, fin, gath, dec, had,
    tsem, wsem, csem, crsem, ysem, yrsem, y2sem, y2rsem, xsem, xrsem, asem, arsem, osem, orsem, ksem,
):
    i, j = lax.axis_index("emit"), lax.axis_index("elem")
    y, x, c = j // 4, j // 2 % 2, j % 2
    nemit = 8
    edev, mdev, samples = xbuf.shape
    lines = steer_ref.shape[3] // 2
    own_rows = pl.ds(pl.multiple_of(i * edev, edev), edev)

    def at(yy, xx, cc):
        return (i, (yy * 2 + xx) * 2 + cc)

    other_core = at(y, x, 1 - c)
    up, down = at((y + 1) % 4, x, c), at((y + 3) % 4, x, c)
    other_x = at(y, 1 - x, c)

    def emit_peer(q):
        return ((i + q) % nemit, j)

    def member(t):
        return (i + t) % nemit

    def bin_in_block(g, n):
        u, w = 4 * g + n // 2, n % 2
        return u * (1 - w) + w * (16 - u - 8 * (1 - (u + 7) // 8))

    def remote(src, dst, ssem, rsem, device):
        return pltpu.make_async_remote_copy(
            src_ref=src, dst_ref=dst, send_sem=ssem, recv_sem=rsem, device_id=device, device_id_type=MESH
        )

    def load(t):
        return pltpu.make_async_copy(
            steer_ref.at[:, bin_in_block(t // 8, member(t))], wbuf.at[t % SLOTS], wsem.at[t % SLOTS]
        )

    def load_traces(blk):
        part = pl.ds(blk * EBLK, EBLK)
        return pltpu.make_async_copy(traces_ref.at[part], xbuf.at[part], tsem.at[blk])

    def core_copy(t):
        return remote(sendc.at[t], recvc.at[t], csem.at[t], crsem.at[t], other_core)

    def y1_copy(t, d):
        return remote(acc.at[t, pl.ds(2 * d, 2)], recv1.at[t, d], ysem.at[t, d], yrsem.at[t, d], up if d == 0 else down)

    def y2_copy(t, d):
        return remote(fwd.at[t, d], recv2.at[t, d], y2sem.at[t, d], y2rsem.at[t, d], up if d == 0 else down)

    def x_copy(t):
        return remote(totx.at[t], recvx.at[t], xsem.at[t], xrsem.at[t], other_x)

    def a_copy(t):
        return remote(fin.at[t], gath.at[t // nemit, own_rows], asem.at[t], arsem.at[t], emit_peer(t))

    def rows_of(q):
        return pl.ds(pl.multiple_of((i + q) % nemit * edev, edev), edev)

    def o_copy(s, q):
        return remote(dec.at[s, rows_of(q)], out_ref.at[bin_in_block(s, i)], osem.at[s, q], orsem.at[s, q], emit_peer(q))

    nblk = edev // EBLK
    pairs = [
        (codes_hbm, codes_ref), (tri_hbm, tri_ref), (head_hbm, head_ref), (body_hbm.at[0], body_ref.at[0]),
        (body_hbm.at[1], body_ref.at[1]), (order_hbm, order_ref),
    ]
    tables = [pltpu.make_async_copy(a, b, ksem.at[n]) for n, (a, b) in enumerate(pairs)]
    for table in tables[:4]:
        table.start()
    for blk in range(nblk):
        load_traces(blk).start()
    for table in tables[4:]:
        table.start()
    for t in range(6):
        load(t).start()
    barrier = pltpu.get_barrier_semaphore()
    peers = [other_core, up, down, other_x] + [emit_peer(q) for q in range(1, nemit)]
    for peer in peers:
        pl.semaphore_signal(barrier, inc=1, device_id=peer, device_id_type=MESH)

    scale = float(samples) ** -0.5
    for table in tables[:3]:
        table.wait()
    for g in range(2):
        fill_tables(g, codes_ref, head_ref, tri_ref, gain, tab, scale)
    tables[3].wait()

    def first_half(blk, carry):
        load_traces(blk).wait()
        transform(0, blk, i * edev, code_ref, xbuf, body_ref, gain, tab, spec)
        return carry

    lax.fori_loop(0, nblk, first_half, 0)
    pl.semaphore_wait(barrier, len(peers))
    tables[4].wait()

    def product(t, slot, core):
        jj = ((y + SLOT_Y[slot]) % 4 * 2 + SLOT_X[slot]) * 2 + core
        g, n = t // 8, member(t)
        neg = 1 - jj // 8
        whole = 8 * g + n
        flip = (whole + 14) // 16 * (1 - 2 * (n % 2))
        row_pos = (jj - 8 * (1 - neg)) * 8 + n
        row_neg = (16 - jj - (whole + 15) // 16) % 8 * 8 + n + flip
        row = (1 - neg) * row_pos + neg * row_neg
        s = wbuf[t % SLOTS, jj]
        w = jnp.concatenate([s, jnp.concatenate([-s[:, lines:], s[:, :lines]], axis=1)], axis=0)
        return jnp.dot(spec[g, neg, row], w, precision=HIGH, preferred_element_type=jnp.float32)

    def twice(h, data):
        hi = data.astype(jnp.bfloat16)
        lo = (data - hi.astype(jnp.float32)).astype(jnp.bfloat16)
        return jnp.dot(h, hi, preferred_element_type=jnp.float32) + jnp.dot(h, lo, preferred_element_type=jnp.float32)

    def decode(s):
        for q in range(1, nemit):
            a_copy(s * nemit + q).wait_recv()
        dec[s] = twice(had[...], gath[s])
        for q in range(1, nemit):
            o_copy(s, q).start()
        out_ref[bin_in_block(s, i)] = dec[s, own_rows]

    def body(t, carry):
        @pl.when(t + 5 < ROUNDS)
        def _():
            @pl.when(t >= 1)
            def _():
                load(t + 5).start()

        @pl.when(t < ROUNDS)
        def _():
            load(t).wait()
            for slot in range(8):
                sendc[t, slot] = product(t, slot, 1 - c)
            core_copy(t).start()

        @pl.when((t >= LAG_B) & (t < ROUNDS + LAG_B))
        def _():
            u = t - LAG_B
            core_copy(u).wait_recv()
            for slot in range(8):
                acc[u, slot] = product(u, slot, c) + recvc[u, slot]
                if slot == 1:
                    y1_copy(u, 0).start()
                if slot == 3:
                    y1_copy(u, 1).start()

        @pl.when((t >= LAG_C) & (t < ROUNDS + LAG_C))
        def _():
            u = t - LAG_C
            for d in range(2):
                y1_copy(u, d).wait_recv()
                fwd[u, d] = acc[u, 4 + d] + recv1[u, d, 0]
                y2_copy(u, d).start()

        @pl.when((t >= LAG_D) & (t < ROUNDS + LAG_D))
        def _():
            u = t - LAG_D
            for d in range(2):
                y2_copy(u, d).wait_recv()
            tot0 = acc[u, 6] + recv2[u, 0] + recv1[u, 1, 1]
            tot1 = acc[u, 7] + recv2[u, 1] + recv1[u, 0, 1]
            totx[u] = jnp.where(x == 0, tot1, tot0)
            fin[u] = jnp.where(x == 0, tot0, tot1)
            x_copy(u).start()

        @pl.when((t >= LAG_E) & (t < ROUNDS + LAG_E))
        def _():
            u = t - LAG_E
            x_copy(u).wait_recv()
            fin[u] = fin[u] + recvx[u]

            @pl.when(u % nemit == 0)
            def _():
                gath[u // nemit, own_rows] = fin[u]

            @pl.when(u % nemit != 0)
            def _():
                a_copy(u).start()

        @pl.when(t == nemit + LAG_E + 2)
        def _():
            decode(0)

        @pl.when((t < 2 * nblk) & (t % 2 == 1))
        def _():
            transform(1, t // 2, i * edev, code_ref, xbuf, body_ref, gain, tab, spec)

        @pl.when(t == 9)
        def _():
            tables[5].wait()
            both = order_ref[...] & lax.broadcasted_iota(jnp.int32, had.shape, 0)
            for shift in (4, 2, 1):
                both = both ^ (both >> shift)
            had[...] = ((1 - 2 * (both & 1)).astype(jnp.float32) * (had.shape[0] ** -0.5)).astype(jnp.bfloat16)

        return carry

    lax.fori_loop(0, ROUNDS + LAG_E, body, 0)

    decode(1)

    def drain(t, carry):
        core_copy(t).wait_send()
        for d in range(2):
            y1_copy(t, d).wait_send()
            y2_copy(t, d).wait_send()
        x_copy(t).wait_send()
        return carry

    lax.fori_loop(0, ROUNDS, drain, 0)
    for s in range(2):
        for q in range(1, nemit):
            a_copy(s * nemit + q).wait_send()
            o_copy(s, q).wait()


def per_device(traces, codes, code_of, order, steer):
    edev, mdev, samples = traces.shape
    ncode, _, taps = codes.shape
    bins, _, width = steer.shape
    emissions = order.shape[0]
    body, head, tri = dft_tables(samples, taps)
    f32 = jnp.float32
    block = (edev, width)
    dma = pltpu.SemaphoreType.DMA
    vmem = pl.BlockSpec(memory_space=pltpu.VMEM)
    hbm = pl.BlockSpec(memory_space=pl.ANY)
    return pl.pallas_call(
        beam_kernel,
        in_specs=[pl.BlockSpec(memory_space=pltpu.SMEM), hbm, hbm, hbm, hbm, hbm, hbm, hbm],
        out_specs=vmem,
        out_shape=jax.ShapeDtypeStruct((16, edev, width), f32),
        scratch_shapes=[
            pltpu.VMEM(codes.shape, f32),
            pltpu.VMEM(head.shape, f32),
            pltpu.VMEM(tri.shape, f32),
            pltpu.VMEM(body.shape, f32),
            pltpu.VMEM((1, emissions), jnp.int32),
            pltpu.VMEM(traces.shape, f32),
            pltpu.VMEM((2, 4 * QUART, ncode * taps), f32),
            pltpu.VMEM((2, ncode, 4 * QUART, 128), f32),
            pltpu.VMEM((2, 2, QUART, edev, 2 * mdev), f32),
            pltpu.VMEM((SLOTS, 16, mdev, width), f32),
            pltpu.VMEM((ROUNDS, 8) + block, f32),
            pltpu.VMEM((ROUNDS, 8) + block, f32),
            pltpu.VMEM((ROUNDS, 8) + block, f32),
            pltpu.VMEM((ROUNDS, 2, 2) + block, f32),
            pltpu.VMEM((ROUNDS, 2) + block, f32),
            pltpu.VMEM((ROUNDS, 2) + block, f32),
            pltpu.VMEM((ROUNDS,) + block, f32),
            pltpu.VMEM((ROUNDS,) + block, f32),
            pltpu.VMEM((ROUNDS,) + block, f32),
            pltpu.VMEM((2, emissions, width), f32),
            pltpu.VMEM((2, emissions, width), f32),
            pltpu.VMEM((emissions, emissions), jnp.bfloat16),
            dma((edev // EBLK,)), dma((SLOTS,)), dma((ROUNDS,)), dma((ROUNDS,)),
            dma((ROUNDS, 2)), dma((ROUNDS, 2)), dma((ROUNDS, 2)), dma((ROUNDS, 2)),
            dma((ROUNDS,)), dma((ROUNDS,)), dma((ROUNDS,)), dma((ROUNDS,)), dma((2, 8)), dma((2, 8)), dma((6,)),
        ],
        compiler_params=pltpu.CompilerParams(collective_id=0, has_side_effects=True, vmem_limit_bytes=60 << 20),
        name="beams",
    )(
        code_of, codes, head, tri, body, order.reshape(1, emissions), traces,
        steer.reshape(16, bins // 16, mdev, width),
    )


def solution(mesh):
    placed = (P("emit", "elem", None), P(), P(), P(), P(None, "elem", None))
    return jax.shard_map(
        per_device, mesh=mesh, in_specs=placed, out_specs=P("elem", "emit", None), check_vma=False
    )
```

```python
import functools

import numpy as np
import jax
import jax.numpy as jnp
from jax import lax
from jax.experimental import pallas as pl
from jax.experimental.pallas import tpu as pltpu
from jax.sharding import PartitionSpec as P

HIGH = lax.Precision.HIGH
NT = (((1,), (1,)), ((), ()))
MESH = pl.DeviceIdType.MESH
ROUNDS = 16
FLIPS = 3
FAR_FIRST = (2, 6, 3, 5, 4, 1, 7)
LAG_B, LAG_C, LAG_D, LAG_E = 1, 3, 5, 7
SLOTS = 8
SLOT_Y = (2, 1, 2, 3, 1, 3, 0, 0)
SLOT_X = (0, 1, 1, 0, 0, 1, 0, 1)
RESIDUES = ((0, 8, 1, 15, 2, 14, 3, 13), (4, 12, 5, 11, 6, 10, 7, 9))
EBLK = 8
QUART = 64


def dft_tables(samples, taps):
    t = np.arange(taps, samples)
    u = np.arange(taps)
    bodies, heads = [], []
    for g in range(2):
        freq = (16 * np.arange(8)[:, None] + np.array(RESIDUES[g])[None, :]).reshape(-1)
        angle = 2 * np.pi * (freq[:, None] * t[None] % samples) / samples
        cosine, sine, extra = np.cos(angle), np.sin(angle), np.zeros((8, t.size))
        if g == 0:
            top = 2 * np.pi * (128 * t % samples) / samples
            sine[0], extra[0] = np.cos(top), np.sin(top)
        bodies.append(np.concatenate([cosine, sine, extra], 0))
        both = np.concatenate([freq, np.where(freq == 0, -128, -freq)])
        angle = 2 * np.pi * (both[:, None] * u[None] % samples) / samples
        heads.append(np.stack([np.cos(angle), np.sin(angle)]))
    tri = (u[:, None] <= u[None, :]).astype(np.float32)
    return np.stack(bodies).astype(np.float32), np.stack(heads).astype(np.float32), tri


def fill_tables(g, codes_ref, head_ref, tri_ref, gain_ref, tab_ref, scale):
    ncode, _, taps = codes_ref.shape
    cosine, sine = head_ref[g, 0], head_ref[g, 1]
    nrow = 2 * QUART
    for c in range(ncode):
        ci = codes_ref[c, 0:1, :] * scale
        cq = codes_ref[c, 1:2, :] * scale
        a_re = ci * cosine - cq * sine
        a_im = ci * sine + cq * cosine
        p_re = jnp.dot(a_re, tri_ref[...], precision=HIGH, preferred_element_type=jnp.float32)
        p_im = jnp.dot(a_im, tri_ref[...], precision=HIGH, preferred_element_type=jnp.float32)
        lanes = slice(c * taps, (c + 1) * taps)
        gain_ref[g, 0:nrow, lanes] = cosine * p_re + sine * p_im
        gain_ref[g, nrow:, lanes] = cosine * p_im - sine * p_re
        tab_ref[g, c, 0:nrow] = jnp.broadcast_to(p_re[:, taps - 1:], (nrow, 128))
        tab_ref[g, c, nrow:] = jnp.broadcast_to(p_im[:, taps - 1:], (nrow, 128))


def transform(g, blk, first_code, code_ref, x_ref, body_ref, gain_ref, tab_ref, spec_ref):
    _, mdev, samples = x_ref.shape
    ncode, taps = tab_ref.shape[1], gain_ref.shape[2] // tab_ref.shape[1]
    nrow = 2 * QUART
    start = pl.multiple_of(blk * EBLK, EBLK)
    x = x_ref[pl.ds(start, EBLK)].reshape(EBLK * mdev, samples)
    spec = lax.dot_general(body_ref[g], x[:, taps:], NT, precision=HIGH, preferred_element_type=jnp.float32)
    codes = [code_ref[first_code + start + e] for e in range(EBLK)]
    masked = jnp.concatenate(
        [
            jnp.concatenate(
                [x_ref[start + e, :, 0:taps] * (codes[e] == c).astype(jnp.float32) for e in range(EBLK)], axis=0
            )
            for c in range(ncode)
        ],
        axis=1,
    )
    corr = lax.dot_general(gain_ref[g], masked, NT, precision=HIGH, preferred_element_type=jnp.float32)
    first = lax.broadcasted_iota(jnp.int32, (QUART, 128), 0) == 0
    left = lax.broadcasted_iota(jnp.int32, (QUART, 128), 1) < mdev
    for sign in range(2):
        rows = slice(sign * QUART, (sign + 1) * QUART)
        irows = slice(nrow + sign * QUART, nrow + (sign + 1) * QUART)
        planes = []
        for q in range(EBLK // 2):
            lanes = slice(q * 128, (q + 1) * 128)
            xc, xs = spec[0:QUART, lanes], spec[QUART:nrow, lanes]
            cr = jnp.where(left, tab_ref[g, codes[2 * q], rows], tab_ref[g, codes[2 * q + 1], rows])
            ci = jnp.where(left, tab_ref[g, codes[2 * q], irows], tab_ref[g, codes[2 * q + 1], irows])
            if sign == 0:
                xs = jnp.where(first, 0.0, -xs) if g == 0 else -xs
            elif g == 0:
                xc = jnp.where(first, xs, xc)
                xs = jnp.where(first, spec[nrow:nrow + 1, lanes], xs)
            re = xc * cr - xs * ci + corr[rows, lanes]
            im = xc * ci + xs * cr + corr[irows, lanes]
            planes.append(jnp.where(left, re, pltpu.roll(im, 64, 1)))
            planes.append(jnp.where(left, pltpu.roll(re, 64, 1), im))
        spec_ref[g, sign, :, pl.ds(start, EBLK), :] = jnp.swapaxes(jnp.stack(planes, 0), 0, 1)


def beam_kernel(
    code_ref, codes_hbm, head_hbm, tri_hbm, body_hbm, order_hbm, traces_ref, steer_ref, out_ref,
    codes_ref, head_ref, tri_ref, body_ref, order_ref, xbuf, gain, tab, spec, wbuf, sendc, recvc, acc, recv1, recv2, fwd, totx, recvx, fin, gath, dec, had, frecv, facc, frecv1, ffwd, frecv2,
    tsem, wsem, csem, crsem, ysem, yrsem, y2sem, y2rsem, xsem, xrsem, asem, arsem, osem, orsem, ksem,
    fsem, frsem, f1sem, f1rsem, f2sem, f2rsem,
):
    i, j = lax.axis_index("emit"), lax.axis_index("elem")
    y, x, c = j // 4, j // 2 % 2, j % 2
    nemit = 8
    edev, mdev, samples = xbuf.shape
    hrow = edev // 2
    lines = steer_ref.shape[3] // 2
    own_rows = pl.ds(pl.multiple_of(i * edev, edev), edev)

    def at(yy, xx, cc):
        return (i, (yy * 2 + xx) * 2 + cc)

    other_core = at(y, x, 1 - c)
    up, down = at((y + 1) % 4, x, c), at((y + 3) % 4, x, c)
    other_x = at(y, 1 - x, c)

    def emit_peer(q):
        return ((i + q) % nemit, j)

    def member(t):
        return (i + t) % nemit

    def bin_in_block(g, n):
        u, w = 4 * g + n // 2, n % 2
        return u * (1 - w) + w * (16 - u - 8 * (1 - (u + 7) // 8))

    def remote(src, dst, ssem, rsem, device):
        return pltpu.make_async_remote_copy(
            src_ref=src, dst_ref=dst, send_sem=ssem, recv_sem=rsem, device_id=device, device_id_type=MESH
        )

    def load(t):
        return pltpu.make_async_copy(
            steer_ref.at[:, bin_in_block(t // 8, member(t))], wbuf.at[t % SLOTS], wsem.at[t % SLOTS]
        )

    def load_traces(blk):
        part = pl.ds(blk * EBLK, EBLK)
        return pltpu.make_async_copy(traces_ref.at[part], xbuf.at[part], tsem.at[blk])

    def core_copy(t):
        return remote(sendc.at[t], recvc.at[t], csem.at[t], crsem.at[t], other_core)

    def y1_copy(t, d):
        return remote(acc.at[t, pl.ds(2 * d, 2)], recv1.at[t, d], ysem.at[t, d], yrsem.at[t, d], up if d == 0 else down)

    def y2_copy(t, d):
        return remote(fwd.at[t, d], recv2.at[t, d], y2sem.at[t, d], y2rsem.at[t, d], up if d == 0 else down)

    def x_copy(t):
        return remote(totx.at[t], recvx.at[t], xsem.at[t], xrsem.at[t], other_x)

    def flipped(t):
        return (t % 4 == 3) & (t < 4 * FLIPS)

    def f_copy(w):
        t = 4 * w + 3
        return remote(acc.at[t, pl.ds(pl.multiple_of((1 - x) * 4, 4), 4)], frecv.at[w], fsem.at[w], frsem.at[w], other_x)

    def f1_copy(w, d):
        return remote(facc.at[w, pl.ds(2 * d, 2)], frecv1.at[w, d], f1sem.at[w, d], f1rsem.at[w, d], up if d == 0 else down)

    def f2_copy(w, d):
        return remote(ffwd.at[w, d], frecv2.at[w, d], f2sem.at[w, d], f2rsem.at[w, d], up if d == 0 else down)

    def a_copy(t):
        return remote(fin.at[t], gath.at[t // nemit, own_rows], asem.at[t], arsem.at[t], emit_peer(t))

    def rows_of(q):
        return pl.ds(pl.multiple_of((i + q) % nemit * edev, edev), edev)

    def o_copy(s, q):
        return remote(dec.at[s, rows_of(q)], out_ref.at[bin_in_block(s, i)], osem.at[s, q], orsem.at[s, q], emit_peer(q))

    nblk = edev // EBLK
    pairs = [
        (codes_hbm, codes_ref), (tri_hbm, tri_ref), (head_hbm, head_ref), (body_hbm.at[0], body_ref.at[0]),
        (body_hbm.at[1], body_ref.at[1]), (order_hbm, order_ref),
    ]
    tables = [pltpu.make_async_copy(a, b, ksem.at[n]) for n, (a, b) in enumerate(pairs)]
    for table in tables[:4]:
        table.start()
    for blk in range(nblk):
        load_traces(blk).start()
    for table in tables[4:]:
        table.start()
    for t in range(6):
        load(t).start()
    barrier = pltpu.get_barrier_semaphore()
    peers = [other_core, up, down, other_x] + [emit_peer(q) for q in range(1, nemit)]
    for peer in peers:
        pl.semaphore_signal(barrier, inc=1, device_id=peer, device_id_type=MESH)

    scale = float(samples) ** -0.5
    for table in tables[:3]:
        table.wait()
    for g in range(2):
        fill_tables(g, codes_ref, head_ref, tri_ref, gain, tab, scale)
    tables[3].wait()

    def first_half(blk, carry):
        load_traces(blk).wait()
        transform(0, blk, i * edev, code_ref, xbuf, body_ref, gain, tab, spec)
        return carry

    lax.fori_loop(0, nblk, first_half, 0)
    pl.semaphore_wait(barrier, len(peers))
    tables[4].wait()

    def product(t, slot, core):
        jj = ((y + SLOT_Y[slot]) % 4 * 2 + SLOT_X[slot]) * 2 + core
        g, n = t // 8, member(t)
        neg = 1 - jj // 8
        whole = 8 * g + n
        flip = (whole + 14) // 16 * (1 - 2 * (n % 2))
        row_pos = (jj - 8 * (1 - neg)) * 8 + n
        row_neg = (16 - jj - (whole + 15) // 16) % 8 * 8 + n + flip
        row = (1 - neg) * row_pos + neg * row_neg
        s = wbuf[t % SLOTS, jj]
        w = jnp.concatenate([s, jnp.concatenate([-s[:, lines:], s[:, :lines]], axis=1)], axis=0)
        return jnp.dot(spec[g, neg, row], w, precision=HIGH, preferred_element_type=jnp.float32)

    def twice(h, data):
        hi = data.astype(jnp.bfloat16)
        lo = (data - hi.astype(jnp.float32)).astype(jnp.bfloat16)
        return jnp.dot(h, hi, preferred_element_type=jnp.float32) + jnp.dot(h, lo, preferred_element_type=jnp.float32)

    def decode(s):
        for q in range(1, nemit):
            a_copy(s * nemit + q).wait_recv()
        dec[s] = twice(had[...], gath[s])
        for q in FAR_FIRST:
            o_copy(s, q).start()
        out_ref[bin_in_block(s, i)] = dec[s, own_rows]

    def body(t, carry):
        @pl.when(t + 5 < ROUNDS)
        def _():
            @pl.when(t >= 1)
            def _():
                load(t + 5).start()

        @pl.when(t < ROUNDS)
        def _():
            load(t).wait()
            for slot in range(8):
                sendc[t, slot] = product(t, slot, 1 - c)
            core_copy(t).start()

        @pl.when((t >= LAG_B) & (t < ROUNDS + LAG_B))
        def _():
            u = t - LAG_B
            core_copy(u).wait_recv()

            @pl.when(~flipped(u))
            def _():
                for slot in range(8):
                    acc[u, slot] = product(u, slot, c) + recvc[u, slot]
                    if slot == 1 or slot == 3:
                        y1_copy(u, slot // 2).start()

            @pl.when(flipped(u))
            def _():
                for slot in range(8):
                    acc[u, SLOT_X[slot] * 4 + SLOT_Y[slot]] = product(u, slot, c) + recvc[u, slot]
                f_copy(u // 4).start()

        @pl.when((t >= LAG_C) & (t < ROUNDS + LAG_C))
        def _():
            u = t - LAG_C
            w = u // 4

            @pl.when(~flipped(u))
            def _():
                for d in range(2):
                    y1_copy(u, d).wait_recv()
                    fwd[u, d] = acc[u, 4 + d] + recv1[u, d, 0]
                    y2_copy(u, d).start()

            @pl.when(flipped(u))
            def _():
                f_copy(w).wait_recv()
                for slot in range(8):
                    rows = slice(SLOT_X[slot] * hrow, (SLOT_X[slot] + 1) * hrow)
                    facc[w, slot] = acc[u, x * 4 + SLOT_Y[slot], rows] + frecv[w, SLOT_Y[slot], rows]
                    if slot == 1 or slot == 3:
                        f1_copy(w, slot // 2).start()

        @pl.when((t >= LAG_D) & (t < ROUNDS + LAG_D))
        def _():
            u = t - LAG_D
            w = u // 4

            @pl.when(~flipped(u))
            def _():
                for d in range(2):
                    y2_copy(u, d).wait_recv()
                tot0 = acc[u, 6] + recv2[u, 0] + recv1[u, 1, 1]
                tot1 = acc[u, 7] + recv2[u, 1] + recv1[u, 0, 1]
                totx[u] = jnp.where(x == 0, tot1, tot0)
                fin[u] = jnp.where(x == 0, tot0, tot1)
                x_copy(u).start()

            @pl.when(flipped(u))
            def _():
                for d in range(2):
                    f1_copy(w, d).wait_recv()
                    ffwd[w, d] = facc[w, 4 + d] + frecv1[w, d, 0]
                    f2_copy(w, d).start()

        @pl.when((t >= LAG_E) & (t < ROUNDS + LAG_E))
        def _():
            u = t - LAG_E
            w = u // 4

            @pl.when(~flipped(u))
            def _():
                x_copy(u).wait_recv()
                fin[u] = fin[u] + recvx[u]

            @pl.when(flipped(u))
            def _():
                for d in range(2):
                    f2_copy(w, d).wait_recv()
                fin[u, 0:hrow] = facc[w, 6] + frecv2[w, 0] + frecv1[w, 1, 1]
                fin[u, hrow:] = facc[w, 7] + frecv2[w, 1] + frecv1[w, 0, 1]


            @pl.when(u % nemit == 0)
            def _():
                gath[u // nemit, own_rows] = fin[u]

            @pl.when(u % nemit != 0)
            def _():
                a_copy(u).start()

        @pl.when(t == nemit + LAG_E + 2)
        def _():
            decode(0)

        @pl.when((t < 2 * nblk) & (t % 2 == 1))
        def _():
            transform(1, t // 2, i * edev, code_ref, xbuf, body_ref, gain, tab, spec)

        @pl.when(t == 9)
        def _():
            tables[5].wait()
            both = order_ref[...] & lax.broadcasted_iota(jnp.int32, had.shape, 0)
            for shift in (4, 2, 1):
                both = both ^ (both >> shift)
            had[...] = ((1 - 2 * (both & 1)).astype(jnp.float32) * (had.shape[0] ** -0.5)).astype(jnp.bfloat16)

        return carry

    lax.fori_loop(0, ROUNDS + LAG_E, body, 0)

    decode(1)

    def drain(t, carry):
        core_copy(t).wait_send()

        @pl.when(~flipped(t))
        def _():
            for d in range(2):
                y1_copy(t, d).wait_send()
                y2_copy(t, d).wait_send()
            x_copy(t).wait_send()

        return carry

    lax.fori_loop(0, ROUNDS, drain, 0)
    for w in range(FLIPS):
        f_copy(w).wait_send()
        for d in range(2):
            f1_copy(w, d).wait_send()
            f2_copy(w, d).wait_send()
    for s in range(2):
        for q in range(1, nemit):
            a_copy(s * nemit + q).wait_send()
            o_copy(s, q).wait()


def per_device(traces, codes, code_of, order, steer):
    edev, mdev, samples = traces.shape
    ncode, _, taps = codes.shape
    bins, _, width = steer.shape
    emissions = order.shape[0]
    body, head, tri = dft_tables(samples, taps)
    f32 = jnp.float32
    block, halved = (edev, width), (edev // 2, width)
    dma = pltpu.SemaphoreType.DMA
    vmem = pl.BlockSpec(memory_space=pltpu.VMEM)
    hbm = pl.BlockSpec(memory_space=pl.ANY)
    return pl.pallas_call(
        beam_kernel,
        in_specs=[pl.BlockSpec(memory_space=pltpu.SMEM), hbm, hbm, hbm, hbm, hbm, hbm, hbm],
        out_specs=vmem,
        out_shape=jax.ShapeDtypeStruct((16, edev, width), f32),
        scratch_shapes=[
            pltpu.VMEM(codes.shape, f32),
            pltpu.VMEM(head.shape, f32),
            pltpu.VMEM(tri.shape, f32),
            pltpu.VMEM(body.shape, f32),
            pltpu.VMEM((1, emissions), jnp.int32),
            pltpu.VMEM(traces.shape, f32),
            pltpu.VMEM((2, 4 * QUART, ncode * taps), f32),
            pltpu.VMEM((2, ncode, 4 * QUART, 128), f32),
            pltpu.VMEM((2, 2, QUART, edev, 2 * mdev), f32),
            pltpu.VMEM((SLOTS, 16, mdev, width), f32),
            pltpu.VMEM((ROUNDS, 8) + block, f32),
            pltpu.VMEM((ROUNDS, 8) + block, f32),
            pltpu.VMEM((ROUNDS, 8) + block, f32),
            pltpu.VMEM((ROUNDS, 2, 2) + block, f32),
            pltpu.VMEM((ROUNDS, 2) + block, f32),
            pltpu.VMEM((ROUNDS, 2) + block, f32),
            pltpu.VMEM((ROUNDS,) + block, f32),
            pltpu.VMEM((ROUNDS,) + block, f32),
            pltpu.VMEM((ROUNDS,) + block, f32),
            pltpu.VMEM((2, emissions, width), f32),
            pltpu.VMEM((2, emissions, width), f32),
            pltpu.VMEM((emissions, emissions), jnp.bfloat16),
            pltpu.VMEM((FLIPS, 4) + block, f32),
            pltpu.VMEM((FLIPS, 8) + halved, f32),
            pltpu.VMEM((FLIPS, 2, 2) + halved, f32),
            pltpu.VMEM((FLIPS, 2) + halved, f32),
            pltpu.VMEM((FLIPS, 2) + halved, f32),
            dma((edev // EBLK,)), dma((SLOTS,)), dma((ROUNDS,)), dma((ROUNDS,)),
            dma((ROUNDS, 2)), dma((ROUNDS, 2)), dma((ROUNDS, 2)), dma((ROUNDS, 2)),
            dma((ROUNDS,)), dma((ROUNDS,)), dma((ROUNDS,)), dma((ROUNDS,)), dma((2, 8)), dma((2, 8)), dma((6,)),
            dma((FLIPS,)), dma((FLIPS,)), dma((FLIPS, 2)), dma((FLIPS, 2)), dma((FLIPS, 2)), dma((FLIPS, 2)),
        ],
        compiler_params=pltpu.CompilerParams(collective_id=0, has_side_effects=True, vmem_limit_bytes=60 << 20),
        name="beams",
    )(
        code_of, codes, head, tri, body, order.reshape(1, emissions), traces,
        steer.reshape(16, bins // 16, mdev, width),
    )


def solution(mesh):
    placed = (P("emit", "elem", None), P(), P(), P(), P(None, "elem", None))
    return jax.shard_map(
        per_device, mesh=mesh, in_specs=placed, out_specs=P("elem", "emit", None), check_vma=False
    )
```

```python
import functools

import numpy as np
import jax
import jax.numpy as jnp
from jax import lax
from jax.experimental import pallas as pl
from jax.experimental.pallas import tpu as pltpu
from jax.sharding import PartitionSpec as P

HIGH = lax.Precision.HIGH
NT = (((1,), (1,)), ((), ()))
MESH = pl.DeviceIdType.MESH
ROUNDS = 16
FLIPS = 3
FAR_FIRST = (2, 6, 3, 5, 4, 1, 7)
LAG_B, LAG_C, LAG_D, LAG_E = 1, 3, 5, 7
SLOTS = 8
SLOT_Y = (2, 1, 2, 3, 1, 3, 0, 0)
SLOT_X = (0, 1, 1, 0, 0, 1, 0, 1)
RESIDUES = ((0, 8, 1, 15, 2, 14, 3, 13), (4, 12, 5, 11, 6, 10, 7, 9))
EBLK = 8
QUART = 64


def dft_tables(samples, taps):
    t = np.arange(taps, samples)
    u = np.arange(taps)
    bodies, heads = [], []
    for g in range(2):
        freq = (16 * np.arange(8)[:, None] + np.array(RESIDUES[g])[None, :]).reshape(-1)
        angle = 2 * np.pi * (freq[:, None] * t[None] % samples) / samples
        cosine, sine, extra = np.cos(angle), np.sin(angle), np.zeros((8, t.size))
        if g == 0:
            top = 2 * np.pi * (128 * t % samples) / samples
            sine[0], extra[0] = np.cos(top), np.sin(top)
        bodies.append(np.concatenate([cosine, sine, extra], 0))
        both = np.concatenate([freq, np.where(freq == 0, -128, -freq)])
        angle = 2 * np.pi * (both[:, None] * u[None] % samples) / samples
        heads.append(np.stack([np.cos(angle), np.sin(angle)]))
    tri = (u[:, None] <= u[None, :]).astype(np.float32)
    return np.stack(bodies).astype(np.float32), np.stack(heads).astype(np.float32), tri


def fill_tables(g, codes_ref, head_ref, tri_ref, gain_ref, tab_ref, scale):
    ncode, _, taps = codes_ref.shape
    cosine, sine = head_ref[g, 0], head_ref[g, 1]
    nrow = 2 * QUART
    for c in range(ncode):
        ci = codes_ref[c, 0:1, :] * scale
        cq = codes_ref[c, 1:2, :] * scale
        a_re = ci * cosine - cq * sine
        a_im = ci * sine + cq * cosine
        p_re = jnp.dot(a_re, tri_ref[...], precision=HIGH, preferred_element_type=jnp.float32)
        p_im = jnp.dot(a_im, tri_ref[...], precision=HIGH, preferred_element_type=jnp.float32)
        lanes = slice(c * taps, (c + 1) * taps)
        gain_ref[g, 0:nrow, lanes] = cosine * p_re + sine * p_im
        gain_ref[g, nrow:, lanes] = cosine * p_im - sine * p_re
        tab_ref[g, c, 0:nrow] = jnp.broadcast_to(p_re[:, taps - 1:], (nrow, 128))
        tab_ref[g, c, nrow:] = jnp.broadcast_to(p_im[:, taps - 1:], (nrow, 128))


def transform(g, blk, first_code, code_ref, x_ref, body_ref, gain_ref, tab_ref, spec_ref):
    _, mdev, samples = x_ref.shape
    ncode, taps = tab_ref.shape[1], gain_ref.shape[2] // tab_ref.shape[1]
    nrow = 2 * QUART
    start = pl.multiple_of(blk * EBLK, EBLK)
    x = x_ref[pl.ds(start, EBLK)].reshape(EBLK * mdev, samples)
    spec = lax.dot_general(body_ref[g], x[:, taps:], NT, precision=HIGH, preferred_element_type=jnp.float32)
    codes = [code_ref[first_code + start + e] for e in range(EBLK)]
    masked = jnp.concatenate(
        [
            jnp.concatenate(
                [x_ref[start + e, :, 0:taps] * (codes[e] == c).astype(jnp.float32) for e in range(EBLK)], axis=0
            )
            for c in range(ncode)
        ],
        axis=1,
    )
    corr = lax.dot_general(gain_ref[g], masked, NT, precision=HIGH, preferred_element_type=jnp.float32)
    first = lax.broadcasted_iota(jnp.int32, (QUART, 128), 0) == 0
    left = lax.broadcasted_iota(jnp.int32, (QUART, 128), 1) < mdev
    for sign in range(2):
        rows = slice(sign * QUART, (sign + 1) * QUART)
        irows = slice(nrow + sign * QUART, nrow + (sign + 1) * QUART)
        planes = []
        for q in range(EBLK // 2):
            lanes = slice(q * 128, (q + 1) * 128)
            xc, xs = spec[0:QUART, lanes], spec[QUART:nrow, lanes]
            cr = jnp.where(left, tab_ref[g, codes[2 * q], rows], tab_ref[g, codes[2 * q + 1], rows])
            ci = jnp.where(left, tab_ref[g, codes[2 * q], irows], tab_ref[g, codes[2 * q + 1], irows])
            if sign == 0:
                xs = jnp.where(first, 0.0, -xs) if g == 0 else -xs
            elif g == 0:
                xc = jnp.where(first, xs, xc)
                xs = jnp.where(first, spec[nrow:nrow + 1, lanes], xs)
            re = xc * cr - xs * ci + corr[rows, lanes]
            im = xc * ci + xs * cr + corr[irows, lanes]
            planes.append(jnp.where(left, re, pltpu.roll(im, 64, 1)))
            planes.append(jnp.where(left, pltpu.roll(re, 64, 1), im))
        spec_ref[g, sign, :, pl.ds(start, EBLK), :] = jnp.swapaxes(jnp.stack(planes, 0), 0, 1)


def beam_kernel(
    code_ref, codes_hbm, head_hbm, tri_hbm, body_hbm, order_hbm, traces_ref, steer_ref, out_ref,
    codes_ref, head_ref, tri_ref, body_ref, order_ref, xbuf, gain, tab, spec, wbuf, sendc, recvc, acc, recv1, recv2, fwd, totx, recvx, fin, gath, dec, had, frecv, facc, frecv1, ffwd, frecv2,
    tsem, wsem, csem, crsem, ysem, yrsem, y2sem, y2rsem, xsem, xrsem, asem, arsem, osem, orsem, ksem,
    fsem, frsem, f1sem, f1rsem, f2sem, f2rsem,
):
    i, j = lax.axis_index("emit"), lax.axis_index("elem")
    y, x, c = j // 4, j // 2 % 2, j % 2
    nemit = 8
    edev, mdev, samples = xbuf.shape
    hrow = edev // 2
    lines = steer_ref.shape[3] // 2
    own_rows = pl.ds(pl.multiple_of(i * edev, edev), edev)

    def at(yy, xx, cc):
        return (i, (yy * 2 + xx) * 2 + cc)

    other_core = at(y, x, 1 - c)
    up, down = at((y + 1) % 4, x, c), at((y + 3) % 4, x, c)
    other_x = at(y, 1 - x, c)

    def emit_peer(q):
        return ((i + q) % nemit, j)

    def member(t):
        return (i + t) % nemit

    def bin_in_block(g, n):
        u, w = 4 * g + n // 2, n % 2
        return u * (1 - w) + w * (16 - u - 8 * (1 - (u + 7) // 8))

    def remote(src, dst, ssem, rsem, device):
        return pltpu.make_async_remote_copy(
            src_ref=src, dst_ref=dst, send_sem=ssem, recv_sem=rsem, device_id=device, device_id_type=MESH
        )

    def load(t):
        return pltpu.make_async_copy(
            steer_ref.at[:, bin_in_block(t // 8, member(t))], wbuf.at[t % SLOTS], wsem.at[t % SLOTS]
        )

    def load_traces(blk):
        part = pl.ds(blk * EBLK, EBLK)
        return pltpu.make_async_copy(traces_ref.at[part], xbuf.at[part], tsem.at[blk])

    def core_copy(t):
        return remote(sendc.at[t], recvc.at[t], csem.at[t], crsem.at[t], other_core)

    def y1_copy(t, d):
        return remote(acc.at[t, pl.ds(2 * d, 2)], recv1.at[t, d], ysem.at[t, d], yrsem.at[t, d], up if d == 0 else down)

    def y2_copy(t, d):
        return remote(fwd.at[t, d], recv2.at[t, d], y2sem.at[t, d], y2rsem.at[t, d], up if d == 0 else down)

    def x_copy(t):
        return remote(totx.at[t], recvx.at[t], xsem.at[t], xrsem.at[t], other_x)

    def flipped(t):
        return (t % 4 == 3) & (t < 4 * FLIPS)

    def f_copy(w):
        t = 4 * w + 3
        return remote(acc.at[t, pl.ds(pl.multiple_of((1 - x) * 4, 4), 4)], frecv.at[w], fsem.at[w], frsem.at[w], other_x)

    def f1_copy(w, d):
        return remote(facc.at[w, pl.ds(2 * d, 2)], frecv1.at[w, d], f1sem.at[w, d], f1rsem.at[w, d], up if d == 0 else down)

    def f2_copy(w, d):
        return remote(ffwd.at[w, d], frecv2.at[w, d], f2sem.at[w, d], f2rsem.at[w, d], up if d == 0 else down)

    def a_copy(t):
        return remote(fin.at[t], gath.at[t // nemit, own_rows], asem.at[t], arsem.at[t], emit_peer(t))

    def rows_of(q):
        return pl.ds(pl.multiple_of((i + q) % nemit * edev, edev), edev)

    def o_copy(s, q):
        return remote(dec.at[s, rows_of(q)], out_ref.at[bin_in_block(s, i)], osem.at[s, q], orsem.at[s, q], emit_peer(q))

    nblk = edev // EBLK
    pairs = [
        (codes_hbm, codes_ref), (tri_hbm, tri_ref), (head_hbm, head_ref), (body_hbm.at[0], body_ref.at[0]),
        (body_hbm.at[1], body_ref.at[1]), (order_hbm, order_ref),
    ]
    tables = [pltpu.make_async_copy(a, b, ksem.at[n]) for n, (a, b) in enumerate(pairs)]
    for table in tables[:4]:
        table.start()
    for blk in range(nblk):
        load_traces(blk).start()
    for table in tables[4:]:
        table.start()
    for t in range(6):
        load(t).start()
    barrier = pltpu.get_barrier_semaphore()
    peers = [other_core, up, down, other_x] + [emit_peer(q) for q in range(1, nemit)]
    for peer in peers:
        pl.semaphore_signal(barrier, inc=1, device_id=peer, device_id_type=MESH)

    scale = float(samples) ** -0.5
    for table in tables[:3]:
        table.wait()
    for g in range(2):
        fill_tables(g, codes_ref, head_ref, tri_ref, gain, tab, scale)
    tables[3].wait()

    def first_half(blk, carry):
        load_traces(blk).wait()
        transform(0, blk, i * edev, code_ref, xbuf, body_ref, gain, tab, spec)
        return carry

    lax.fori_loop(0, nblk, first_half, 0)
    pl.semaphore_wait(barrier, len(peers))
    tables[4].wait()

    def product(t, slot, core):
        jj = ((y + SLOT_Y[slot]) % 4 * 2 + SLOT_X[slot]) * 2 + core
        g, n = t // 8, member(t)
        neg = 1 - jj // 8
        whole = 8 * g + n
        flip = (whole + 14) // 16 * (1 - 2 * (n % 2))
        row_pos = (jj - 8 * (1 - neg)) * 8 + n
        row_neg = (16 - jj - (whole + 15) // 16) % 8 * 8 + n + flip
        row = (1 - neg) * row_pos + neg * row_neg
        s = wbuf[t % SLOTS, jj]
        d = spec[g, neg, row]
        w_hi = s.astype(jnp.bfloat16)
        w_lo = (s - w_hi.astype(jnp.float32)).astype(jnp.bfloat16)
        d_hi = d.astype(jnp.bfloat16)
        d_lo = (d - d_hi.astype(jnp.float32)).astype(jnp.bfloat16)
        turn = lambda v: jnp.concatenate([-v[:, lines:], v[:, :lines]], axis=1)
        left = jnp.concatenate([jnp.concatenate([d_hi, d_hi], axis=1), jnp.concatenate([d_lo, jnp.zeros_like(d_lo)], axis=1)], axis=0)
        right = jnp.concatenate([w_hi, turn(w_hi), w_lo, turn(w_lo)], axis=0)
        both = jnp.dot(left, right, preferred_element_type=jnp.float32)
        return both[:edev] + both[edev:]

    def twice(h, data):
        hi = data.astype(jnp.bfloat16)
        lo = (data - hi.astype(jnp.float32)).astype(jnp.bfloat16)
        return jnp.dot(h, hi, preferred_element_type=jnp.float32) + jnp.dot(h, lo, preferred_element_type=jnp.float32)

    def decode(s):
        for q in range(1, nemit):
            a_copy(s * nemit + q).wait_recv()
        dec[s] = twice(had[...], gath[s])
        for q in FAR_FIRST:
            o_copy(s, q).start()
        out_ref[bin_in_block(s, i)] = dec[s, own_rows]

    def body(t, carry):
        @pl.when(t + 5 < ROUNDS)
        def _():
            @pl.when(t >= 1)
            def _():
                load(t + 5).start()

        @pl.when(t < ROUNDS)
        def _():
            load(t).wait()
            for slot in range(8):
                sendc[t, slot] = product(t, slot, 1 - c)
            core_copy(t).start()

        @pl.when((t >= LAG_B) & (t < ROUNDS + LAG_B))
        def _():
            u = t - LAG_B
            core_copy(u).wait_recv()

            @pl.when(~flipped(u))
            def _():
                for slot in range(8):
                    acc[u, slot] = product(u, slot, c) + recvc[u, slot]
                    if slot == 1 or slot == 3:
                        y1_copy(u, slot // 2).start()

            @pl.when(flipped(u))
            def _():
                for slot in range(8):
                    acc[u, SLOT_X[slot] * 4 + SLOT_Y[slot]] = product(u, slot, c) + recvc[u, slot]
                f_copy(u // 4).start()

        @pl.when((t >= LAG_C) & (t < ROUNDS + LAG_C))
        def _():
            u = t - LAG_C
            w = u // 4

            @pl.when(~flipped(u))
            def _():
                for d in range(2):
                    y1_copy(u, d).wait_recv()
                    fwd[u, d] = acc[u, 4 + d] + recv1[u, d, 0]
                    y2_copy(u, d).start()

            @pl.when(flipped(u))
            def _():
                f_copy(w).wait_recv()
                for slot in range(8):
                    rows = slice(SLOT_X[slot] * hrow, (SLOT_X[slot] + 1) * hrow)
                    facc[w, slot] = acc[u, x * 4 + SLOT_Y[slot], rows] + frecv[w, SLOT_Y[slot], rows]
                    if slot == 1 or slot == 3:
                        f1_copy(w, slot // 2).start()

        @pl.when((t >= LAG_D) & (t < ROUNDS + LAG_D))
        def _():
            u = t - LAG_D
            w = u // 4

            @pl.when(~flipped(u))
            def _():
                for d in range(2):
                    y2_copy(u, d).wait_recv()
                tot0 = acc[u, 6] + recv2[u, 0] + recv1[u, 1, 1]
                tot1 = acc[u, 7] + recv2[u, 1] + recv1[u, 0, 1]
                totx[u] = jnp.where(x == 0, tot1, tot0)
                fin[u] = jnp.where(x == 0, tot0, tot1)
                x_copy(u).start()

            @pl.when(flipped(u))
            def _():
                for d in range(2):
                    f1_copy(w, d).wait_recv()
                    ffwd[w, d] = facc[w, 4 + d] + frecv1[w, d, 0]
                    f2_copy(w, d).start()

        @pl.when((t >= LAG_E) & (t < ROUNDS + LAG_E))
        def _():
            u = t - LAG_E
            w = u // 4

            @pl.when(~flipped(u))
            def _():
                x_copy(u).wait_recv()
                fin[u] = fin[u] + recvx[u]

            @pl.when(flipped(u))
            def _():
                for d in range(2):
                    f2_copy(w, d).wait_recv()
                fin[u, 0:hrow] = facc[w, 6] + frecv2[w, 0] + frecv1[w, 1, 1]
                fin[u, hrow:] = facc[w, 7] + frecv2[w, 1] + frecv1[w, 0, 1]


            @pl.when(u % nemit == 0)
            def _():
                gath[u // nemit, own_rows] = fin[u]

            @pl.when(u % nemit != 0)
            def _():
                a_copy(u).start()

        @pl.when(t == nemit + LAG_E + 2)
        def _():
            decode(0)

        @pl.when((t < 2 * nblk) & (t % 2 == 1))
        def _():
            transform(1, t // 2, i * edev, code_ref, xbuf, body_ref, gain, tab, spec)

        @pl.when(t == 9)
        def _():
            tables[5].wait()
            both = order_ref[...] & lax.broadcasted_iota(jnp.int32, had.shape, 0)
            for shift in (4, 2, 1):
                both = both ^ (both >> shift)
            had[...] = ((1 - 2 * (both & 1)).astype(jnp.float32) * (had.shape[0] ** -0.5)).astype(jnp.bfloat16)

        return carry

    lax.fori_loop(0, ROUNDS + LAG_E, body, 0)

    decode(1)

    def drain(t, carry):
        core_copy(t).wait_send()

        @pl.when(~flipped(t))
        def _():
            for d in range(2):
                y1_copy(t, d).wait_send()
                y2_copy(t, d).wait_send()
            x_copy(t).wait_send()

        return carry

    lax.fori_loop(0, ROUNDS, drain, 0)
    for w in range(FLIPS):
        f_copy(w).wait_send()
        for d in range(2):
            f1_copy(w, d).wait_send()
            f2_copy(w, d).wait_send()
    for s in range(2):
        for q in range(1, nemit):
            a_copy(s * nemit + q).wait_send()
            o_copy(s, q).wait()


def per_device(traces, codes, code_of, order, steer):
    edev, mdev, samples = traces.shape
    ncode, _, taps = codes.shape
    bins, _, width = steer.shape
    emissions = order.shape[0]
    body, head, tri = dft_tables(samples, taps)
    f32 = jnp.float32
    block, halved = (edev, width), (edev // 2, width)
    dma = pltpu.SemaphoreType.DMA
    vmem = pl.BlockSpec(memory_space=pltpu.VMEM)
    hbm = pl.BlockSpec(memory_space=pl.ANY)
    return pl.pallas_call(
        beam_kernel,
        in_specs=[pl.BlockSpec(memory_space=pltpu.SMEM), hbm, hbm, hbm, hbm, hbm, hbm, hbm],
        out_specs=vmem,
        out_shape=jax.ShapeDtypeStruct((16, edev, width), f32),
        scratch_shapes=[
            pltpu.VMEM(codes.shape, f32),
            pltpu.VMEM(head.shape, f32),
            pltpu.VMEM(tri.shape, f32),
            pltpu.VMEM(body.shape, f32),
            pltpu.VMEM((1, emissions), jnp.int32),
            pltpu.VMEM(traces.shape, f32),
            pltpu.VMEM((2, 4 * QUART, ncode * taps), f32),
            pltpu.VMEM((2, ncode, 4 * QUART, 128), f32),
            pltpu.VMEM((2, 2, QUART, edev, 2 * mdev), f32),
            pltpu.VMEM((SLOTS, 16, mdev, width), f32),
            pltpu.VMEM((ROUNDS, 8) + block, f32),
            pltpu.VMEM((ROUNDS, 8) + block, f32),
            pltpu.VMEM((ROUNDS, 8) + block, f32),
            pltpu.VMEM((ROUNDS, 2, 2) + block, f32),
            pltpu.VMEM((ROUNDS, 2) + block, f32),
            pltpu.VMEM((ROUNDS, 2) + block, f32),
            pltpu.VMEM((ROUNDS,) + block, f32),
            pltpu.VMEM((ROUNDS,) + block, f32),
            pltpu.VMEM((ROUNDS,) + block, f32),
            pltpu.VMEM((2, emissions, width), f32),
            pltpu.VMEM((2, emissions, width), f32),
            pltpu.VMEM((emissions, emissions), jnp.bfloat16),
            pltpu.VMEM((FLIPS, 4) + block, f32),
            pltpu.VMEM((FLIPS, 8) + halved, f32),
            pltpu.VMEM((FLIPS, 2, 2) + halved, f32),
            pltpu.VMEM((FLIPS, 2) + halved, f32),
            pltpu.VMEM((FLIPS, 2) + halved, f32),
            dma((edev // EBLK,)), dma((SLOTS,)), dma((ROUNDS,)), dma((ROUNDS,)),
            dma((ROUNDS, 2)), dma((ROUNDS, 2)), dma((ROUNDS, 2)), dma((ROUNDS, 2)),
            dma((ROUNDS,)), dma((ROUNDS,)), dma((ROUNDS,)), dma((ROUNDS,)), dma((2, 8)), dma((2, 8)), dma((6,)),
            dma((FLIPS,)), dma((FLIPS,)), dma((FLIPS, 2)), dma((FLIPS, 2)), dma((FLIPS, 2)), dma((FLIPS, 2)),
        ],
        compiler_params=pltpu.CompilerParams(collective_id=0, has_side_effects=True, vmem_limit_bytes=60 << 20),
        name="beams",
    )(
        code_of, codes, head, tri, body, order.reshape(1, emissions), traces,
        steer.reshape(16, bins // 16, mdev, width),
    )


def solution(mesh):
    placed = (P("emit", "elem", None), P(), P(), P(), P(None, "elem", None))
    return jax.shard_map(
        per_device, mesh=mesh, in_specs=placed, out_specs=P("elem", "emit", None), check_vma=False
    )
```

```python
import functools

import numpy as np
import jax
import jax.numpy as jnp
from jax import lax
from jax.experimental import pallas as pl
from jax.experimental.pallas import tpu as pltpu
from jax.sharding import PartitionSpec as P

HIGH = lax.Precision.HIGH
NT = (((1,), (1,)), ((), ()))
MESH = pl.DeviceIdType.MESH
ROUNDS = 16
FLIPS = 3
FAR_FIRST = (2, 6, 3, 5, 4, 1, 7)
LAG_B, LAG_C, LAG_D, LAG_E = 1, 3, 5, 7
SLOTS = 8
SLOT_Y = (2, 1, 2, 3, 1, 3, 0, 0)
SLOT_X = (0, 1, 1, 0, 0, 1, 0, 1)
RESIDUES = ((0, 8, 1, 15, 2, 14, 3, 13), (4, 12, 5, 11, 6, 10, 7, 9))
EBLK = 8
QUART = 64


def dft_tables(samples, taps):
    t = np.arange(taps, samples)
    u = np.arange(taps)
    bodies, heads = [], []
    for g in range(2):
        freq = (16 * np.arange(8)[:, None] + np.array(RESIDUES[g])[None, :]).reshape(-1)
        angle = 2 * np.pi * (freq[:, None] * t[None] % samples) / samples
        cosine, sine, extra = np.cos(angle), np.sin(angle), np.zeros((8, t.size))
        if g == 0:
            top = 2 * np.pi * (128 * t % samples) / samples
            sine[0], extra[0] = np.cos(top), np.sin(top)
        bodies.append(np.concatenate([cosine, sine, extra], 0))
        both = np.concatenate([freq, np.where(freq == 0, -128, -freq)])
        angle = 2 * np.pi * (both[:, None] * u[None] % samples) / samples
        heads.append(np.stack([np.cos(angle), np.sin(angle)]))
    tri = (u[:, None] <= u[None, :]).astype(np.float32)
    return np.stack(bodies).astype(np.float32), np.stack(heads).astype(np.float32), tri


def fill_tables(g, codes_ref, head_ref, tri_ref, gain_ref, tab_ref, scale):
    ncode, _, taps = codes_ref.shape
    cosine, sine = head_ref[g, 0], head_ref[g, 1]
    nrow = 2 * QUART
    for c in range(ncode):
        ci = codes_ref[c, 0:1, :] * scale
        cq = codes_ref[c, 1:2, :] * scale
        a_re = ci * cosine - cq * sine
        a_im = ci * sine + cq * cosine
        p_re = jnp.dot(a_re, tri_ref[...], precision=HIGH, preferred_element_type=jnp.float32)
        p_im = jnp.dot(a_im, tri_ref[...], precision=HIGH, preferred_element_type=jnp.float32)
        lanes = slice(c * taps, (c + 1) * taps)
        gain_ref[g, 0:nrow, lanes] = cosine * p_re + sine * p_im
        gain_ref[g, nrow:, lanes] = cosine * p_im - sine * p_re
        tab_ref[g, c, 0:nrow] = jnp.broadcast_to(p_re[:, taps - 1:], (nrow, 128))
        tab_ref[g, c, nrow:] = jnp.broadcast_to(p_im[:, taps - 1:], (nrow, 128))


def transform(g, blk, first_code, code_ref, x_ref, body_ref, gain_ref, tab_ref, spec_ref):
    _, mdev, samples = x_ref.shape
    ncode, taps = tab_ref.shape[1], gain_ref.shape[2] // tab_ref.shape[1]
    nrow = 2 * QUART
    start = pl.multiple_of(blk * EBLK, EBLK)
    x = x_ref[pl.ds(start, EBLK)].reshape(EBLK * mdev, samples)
    spec = lax.dot_general(body_ref[g], x[:, taps:], NT, precision=HIGH, preferred_element_type=jnp.float32)
    codes = [code_ref[first_code + start + e] for e in range(EBLK)]
    masked = jnp.concatenate(
        [
            jnp.concatenate(
                [x_ref[start + e, :, 0:taps] * (codes[e] == c).astype(jnp.float32) for e in range(EBLK)], axis=0
            )
            for c in range(ncode)
        ],
        axis=1,
    )
    corr = lax.dot_general(gain_ref[g], masked, NT, precision=HIGH, preferred_element_type=jnp.float32)
    first = lax.broadcasted_iota(jnp.int32, (QUART, 128), 0) == 0
    left = lax.broadcasted_iota(jnp.int32, (QUART, 128), 1) < mdev
    for sign in range(2):
        rows = slice(sign * QUART, (sign + 1) * QUART)
        irows = slice(nrow + sign * QUART, nrow + (sign + 1) * QUART)
        planes = []
        for q in range(EBLK // 2):
            lanes = slice(q * 128, (q + 1) * 128)
            xc, xs = spec[0:QUART, lanes], spec[QUART:nrow, lanes]
            cr = jnp.where(left, tab_ref[g, codes[2 * q], rows], tab_ref[g, codes[2 * q + 1], rows])
            ci = jnp.where(left, tab_ref[g, codes[2 * q], irows], tab_ref[g, codes[2 * q + 1], irows])
            if sign == 0:
                xs = jnp.where(first, 0.0, -xs) if g == 0 else -xs
            elif g == 0:
                xc = jnp.where(first, xs, xc)
                xs = jnp.where(first, spec[nrow:nrow + 1, lanes], xs)
            re = xc * cr - xs * ci + corr[rows, lanes]
            im = xc * ci + xs * cr + corr[irows, lanes]
            planes.append(jnp.where(left, re, pltpu.roll(im, 64, 1)))
            planes.append(jnp.where(left, pltpu.roll(re, 64, 1), im))
        spec_ref[g, sign, :, pl.ds(start, EBLK), :] = jnp.swapaxes(jnp.stack(planes, 0), 0, 1)


def beam_kernel(
    code_ref, codes_hbm, head_hbm, tri_hbm, body_hbm, order_hbm, traces_ref, steer_ref, out_ref,
    codes_ref, head_ref, tri_ref, body_ref, order_ref, xbuf, gain, tab, spec, wbuf, sendc, recvc, acc, recv1, recv2, fwd, totx, recvx, fin, gath, dec, had, frecv, facc, frecv1, ffwd, frecv2,
    tsem, wsem, csem, crsem, ysem, yrsem, y2sem, y2rsem, xsem, xrsem, asem, arsem, osem, orsem, ksem,
    fsem, frsem, f1sem, f1rsem, f2sem, f2rsem,
):
    i, j = lax.axis_index("emit"), lax.axis_index("elem")
    y, x, c = j // 4, j // 2 % 2, j % 2
    nemit = 8
    edev, mdev, samples = xbuf.shape
    hrow = edev // 2
    lines = steer_ref.shape[3] // 2
    own_rows = pl.ds(pl.multiple_of(i * edev, edev), edev)

    def at(yy, xx, cc):
        return (i, (yy * 2 + xx) * 2 + cc)

    other_core = at(y, x, 1 - c)
    up, down = at((y + 1) % 4, x, c), at((y + 3) % 4, x, c)
    other_x = at(y, 1 - x, c)

    def emit_peer(q):
        return ((i + q) % nemit, j)

    def member(t):
        return (i + t) % nemit

    def bin_in_block(g, n):
        u, w = 4 * g + n // 2, n % 2
        return u * (1 - w) + w * (16 - u - 8 * (1 - (u + 7) // 8))

    def remote(src, dst, ssem, rsem, device):
        return pltpu.make_async_remote_copy(
            src_ref=src, dst_ref=dst, send_sem=ssem, recv_sem=rsem, device_id=device, device_id_type=MESH
        )

    def load(t):
        return pltpu.make_async_copy(
            steer_ref.at[:, bin_in_block(t // 8, member(t))], wbuf.at[t % SLOTS], wsem.at[t % SLOTS]
        )

    def load_traces(blk):
        part = pl.ds(blk * EBLK, EBLK)
        return pltpu.make_async_copy(traces_ref.at[part], xbuf.at[part], tsem.at[blk])

    def core_copy(t):
        return remote(sendc.at[t], recvc.at[t], csem.at[t], crsem.at[t], other_core)

    def y1_copy(t, d):
        return remote(acc.at[t, pl.ds(2 * d, 2)], recv1.at[t, d], ysem.at[t, d], yrsem.at[t, d], up if d == 0 else down)

    def y2_copy(t, d):
        return remote(fwd.at[t, d], recv2.at[t, d], y2sem.at[t, d], y2rsem.at[t, d], up if d == 0 else down)

    def x_copy(t):
        return remote(totx.at[t], recvx.at[t], xsem.at[t], xrsem.at[t], other_x)

    def flipped(t):
        return (t % 4 == 3) & (t < 4 * FLIPS)

    def f_copy(w):
        t = 4 * w + 3
        return remote(acc.at[t, pl.ds(pl.multiple_of((1 - x) * 4, 4), 4)], frecv.at[w], fsem.at[w], frsem.at[w], other_x)

    def f1_copy(w, d):
        return remote(facc.at[w, pl.ds(2 * d, 2)], frecv1.at[w, d], f1sem.at[w, d], f1rsem.at[w, d], up if d == 0 else down)

    def f2_copy(w, d):
        return remote(ffwd.at[w, d], frecv2.at[w, d], f2sem.at[w, d], f2rsem.at[w, d], up if d == 0 else down)

    def a_copy(t):
        return remote(fin.at[t], gath.at[t // nemit, own_rows], asem.at[t], arsem.at[t], emit_peer(t))

    def rows_of(q):
        return pl.ds(pl.multiple_of((i + q) % nemit * edev, edev), edev)

    def o_copy(s, q):
        return remote(dec.at[s, rows_of(q)], out_ref.at[bin_in_block(s, i)], osem.at[s, q], orsem.at[s, q], emit_peer(q))

    nblk = edev // EBLK
    pairs = [
        (codes_hbm, codes_ref), (tri_hbm, tri_ref), (head_hbm, head_ref), (body_hbm.at[0], body_ref.at[0]),
        (body_hbm.at[1], body_ref.at[1]), (order_hbm, order_ref),
    ]
    tables = [pltpu.make_async_copy(a, b, ksem.at[n]) for n, (a, b) in enumerate(pairs)]
    for table in tables[:4]:
        table.start()
    for blk in range(nblk):
        load_traces(blk).start()
    for table in tables[4:]:
        table.start()
    for t in range(6):
        load(t).start()
    barrier = pltpu.get_barrier_semaphore()
    peers = [other_core, up, down, other_x] + [emit_peer(q) for q in range(1, nemit)]
    for peer in peers:
        pl.semaphore_signal(barrier, inc=1, device_id=peer, device_id_type=MESH)

    scale = float(samples) ** -0.5
    for table in tables[:3]:
        table.wait()
    for g in range(2):
        fill_tables(g, codes_ref, head_ref, tri_ref, gain, tab, scale)
    tables[3].wait()

    def first_half(blk, carry):
        load_traces(blk).wait()
        transform(0, blk, i * edev, code_ref, xbuf, body_ref, gain, tab, spec)
        return carry

    lax.fori_loop(0, nblk, first_half, 0)
    pl.semaphore_wait(barrier, len(peers))
    tables[4].wait()

    def product(t, slot, core):
        jj = ((y + SLOT_Y[slot]) % 4 * 2 + SLOT_X[slot]) * 2 + core
        g, n = t // 8, member(t)
        neg = 1 - jj // 8
        whole = 8 * g + n
        flip = (whole + 14) // 16 * (1 - 2 * (n % 2))
        row_pos = (jj - 8 * (1 - neg)) * 8 + n
        row_neg = (16 - jj - (whole + 15) // 16) % 8 * 8 + n + flip
        row = (1 - neg) * row_pos + neg * row_neg
        s = wbuf[t % SLOTS, jj]
        d = spec[g, neg, row]
        w_hi = s.astype(jnp.bfloat16)
        w_lo = (s - w_hi.astype(jnp.float32)).astype(jnp.bfloat16)
        d_hi = d.astype(jnp.bfloat16)
        d_lo = (d - d_hi.astype(jnp.float32)).astype(jnp.bfloat16)
        turn = lambda v: jnp.concatenate([-v[:, lines:], v[:, :lines]], axis=1)
        left = jnp.concatenate([jnp.concatenate([d_hi, d_hi], axis=1), jnp.concatenate([d_lo, jnp.zeros_like(d_lo)], axis=1)], axis=0)
        right = jnp.concatenate([w_hi, turn(w_hi), w_lo, turn(w_lo)], axis=0)
        both = jnp.dot(left, right, preferred_element_type=jnp.float32)
        return both[:edev] + both[edev:]

    def twice(h, data):
        hi = data.astype(jnp.bfloat16)
        lo = (data - hi.astype(jnp.float32)).astype(jnp.bfloat16)
        return jnp.dot(h, hi, preferred_element_type=jnp.float32) + jnp.dot(h, lo, preferred_element_type=jnp.float32)

    def decode(s):
        for q in range(1, nemit):
            a_copy(s * nemit + q).wait_recv()
        dec[s] = twice(had[...], gath[s])
        for q in FAR_FIRST:
            o_copy(s, q).start()
        out_ref[bin_in_block(s, i)] = dec[s, own_rows]

    def body(t, carry):
        @pl.when(t + 5 < ROUNDS)
        def _():
            @pl.when(t >= 1)
            def _():
                load(t + 5).start()

        @pl.when(t < ROUNDS)
        def _():
            load(t).wait()
            for slot in range(8):
                sendc[t, slot] = product(t, slot, 1 - c)
            core_copy(t).start()

        @pl.when((t >= LAG_B) & (t < ROUNDS + LAG_B))
        def _():
            u = t - LAG_B
            core_copy(u).wait_recv()

            @pl.when(~flipped(u))
            def _():
                for slot in range(8):
                    acc[u, slot] = product(u, slot, c) + recvc[u, slot]
                    if slot == 1 or slot == 3:
                        y1_copy(u, slot // 2).start()

            @pl.when(flipped(u))
            def _():
                for slot in range(8):
                    acc[u, SLOT_X[slot] * 4 + SLOT_Y[slot]] = product(u, slot, c) + recvc[u, slot]
                f_copy(u // 4).start()

        @pl.when((t >= LAG_C) & (t < ROUNDS + LAG_C))
        def _():
            u = t - LAG_C
            w = u // 4

            @pl.when(~flipped(u))
            def _():
                for d in range(2):
                    y1_copy(u, d).wait_recv()
                    fwd[u, d] = acc[u, 4 + d] + recv1[u, d, 0]
                    y2_copy(u, d).start()

            @pl.when(flipped(u))
            def _():
                f_copy(w).wait_recv()
                for slot in range(8):
                    rows = slice(SLOT_X[slot] * hrow, (SLOT_X[slot] + 1) * hrow)
                    facc[w, slot] = acc[u, x * 4 + SLOT_Y[slot], rows] + frecv[w, SLOT_Y[slot], rows]
                    if slot == 1 or slot == 3:
                        f1_copy(w, slot // 2).start()

        @pl.when((t >= LAG_D) & (t < ROUNDS + LAG_D))
        def _():
            u = t - LAG_D
            w = u // 4

            @pl.when(~flipped(u))
            def _():
                for d in range(2):
                    y2_copy(u, d).wait_recv()
                tot0 = acc[u, 6] + recv2[u, 0] + recv1[u, 1, 1]
                tot1 = acc[u, 7] + recv2[u, 1] + recv1[u, 0, 1]
                totx[u] = jnp.where(x == 0, tot1, tot0)
                fin[u] = jnp.where(x == 0, tot0, tot1)
                x_copy(u).start()

            @pl.when(flipped(u))
            def _():
                for d in range(2):
                    f1_copy(w, d).wait_recv()
                    ffwd[w, d] = facc[w, 4 + d] + frecv1[w, d, 0]
                    f2_copy(w, d).start()

        @pl.when((t >= LAG_E) & (t < ROUNDS + LAG_E))
        def _():
            u = t - LAG_E
            w = u // 4

            @pl.when(~flipped(u))
            def _():
                x_copy(u).wait_recv()
                fin[u] = fin[u] + recvx[u]

            @pl.when(flipped(u))
            def _():
                for d in range(2):
                    f2_copy(w, d).wait_recv()
                fin[u, 0:hrow] = facc[w, 6] + frecv2[w, 0] + frecv1[w, 1, 1]
                fin[u, hrow:] = facc[w, 7] + frecv2[w, 1] + frecv1[w, 0, 1]


            @pl.when(u % nemit == 0)
            def _():
                gath[u // nemit, own_rows] = fin[u]

            @pl.when(u % nemit != 0)
            def _():
                a_copy(u).start()

        @pl.when(t == nemit + LAG_E + 2)
        def _():
            decode(0)

        @pl.when((t >= 2) & (t < 8) & (t != 3) & (t != 6))
        def _():
            transform(1, (t - 1) // 2, i * edev, code_ref, xbuf, body_ref, gain, tab, spec)

        @pl.when(t == 9)
        def _():
            tables[5].wait()
            both = order_ref[...] & lax.broadcasted_iota(jnp.int32, had.shape, 0)
            for shift in (4, 2, 1):
                both = both ^ (both >> shift)
            had[...] = ((1 - 2 * (both & 1)).astype(jnp.float32) * (had.shape[0] ** -0.5)).astype(jnp.bfloat16)

        return carry

    lax.fori_loop(0, ROUNDS + LAG_E, body, 0)

    decode(1)

    def drain(t, carry):
        core_copy(t).wait_send()

        @pl.when(~flipped(t))
        def _():
            for d in range(2):
                y1_copy(t, d).wait_send()
                y2_copy(t, d).wait_send()
            x_copy(t).wait_send()

        return carry

    lax.fori_loop(0, ROUNDS, drain, 0)
    for w in range(FLIPS):
        f_copy(w).wait_send()
        for d in range(2):
            f1_copy(w, d).wait_send()
            f2_copy(w, d).wait_send()
    for s in range(2):
        for q in range(1, nemit):
            a_copy(s * nemit + q).wait_send()
            o_copy(s, q).wait()


def per_device(traces, codes, code_of, order, steer):
    edev, mdev, samples = traces.shape
    ncode, _, taps = codes.shape
    bins, _, width = steer.shape
    emissions = order.shape[0]
    body, head, tri = dft_tables(samples, taps)
    f32 = jnp.float32
    block, halved = (edev, width), (edev // 2, width)
    dma = pltpu.SemaphoreType.DMA
    vmem = pl.BlockSpec(memory_space=pltpu.VMEM)
    hbm = pl.BlockSpec(memory_space=pl.ANY)
    return pl.pallas_call(
        beam_kernel,
        in_specs=[pl.BlockSpec(memory_space=pltpu.SMEM), hbm, hbm, hbm, hbm, hbm, hbm, hbm],
        out_specs=vmem,
        out_shape=jax.ShapeDtypeStruct((16, edev, width), f32),
        scratch_shapes=[
            pltpu.VMEM(codes.shape, f32),
            pltpu.VMEM(head.shape, f32),
            pltpu.VMEM(tri.shape, f32),
            pltpu.VMEM(body.shape, f32),
            pltpu.VMEM((1, emissions), jnp.int32),
            pltpu.VMEM(traces.shape, f32),
            pltpu.VMEM((2, 4 * QUART, ncode * taps), f32),
            pltpu.VMEM((2, ncode, 4 * QUART, 128), f32),
            pltpu.VMEM((2, 2, QUART, edev, 2 * mdev), f32),
            pltpu.VMEM((SLOTS, 16, mdev, width), f32),
            pltpu.VMEM((ROUNDS, 8) + block, f32),
            pltpu.VMEM((ROUNDS, 8) + block, f32),
            pltpu.VMEM((ROUNDS, 8) + block, f32),
            pltpu.VMEM((ROUNDS, 2, 2) + block, f32),
            pltpu.VMEM((ROUNDS, 2) + block, f32),
            pltpu.VMEM((ROUNDS, 2) + block, f32),
            pltpu.VMEM((ROUNDS,) + block, f32),
            pltpu.VMEM((ROUNDS,) + block, f32),
            pltpu.VMEM((ROUNDS,) + block, f32),
            pltpu.VMEM((2, emissions, width), f32),
            pltpu.VMEM((2, emissions, width), f32),
            pltpu.VMEM((emissions, emissions), jnp.bfloat16),
            pltpu.VMEM((FLIPS, 4) + block, f32),
            pltpu.VMEM((FLIPS, 8) + halved, f32),
            pltpu.VMEM((FLIPS, 2, 2) + halved, f32),
            pltpu.VMEM((FLIPS, 2) + halved, f32),
            pltpu.VMEM((FLIPS, 2) + halved, f32),
            dma((edev // EBLK,)), dma((SLOTS,)), dma((ROUNDS,)), dma((ROUNDS,)),
            dma((ROUNDS, 2)), dma((ROUNDS, 2)), dma((ROUNDS, 2)), dma((ROUNDS, 2)),
            dma((ROUNDS,)), dma((ROUNDS,)), dma((ROUNDS,)), dma((ROUNDS,)), dma((2, 8)), dma((2, 8)), dma((6,)),
            dma((FLIPS,)), dma((FLIPS,)), dma((FLIPS, 2)), dma((FLIPS, 2)), dma((FLIPS, 2)), dma((FLIPS, 2)),
        ],
        compiler_params=pltpu.CompilerParams(collective_id=0, has_side_effects=True, vmem_limit_bytes=60 << 20),
        name="beams",
    )(
        code_of, codes, head, tri, body, order.reshape(1, emissions), traces,
        steer.reshape(16, bins // 16, mdev, width),
    )


def solution(mesh):
    placed = (P("emit", "elem", None), P(), P(), P(), P(None, "elem", None))
    return jax.shard_map(
        per_device, mesh=mesh, in_specs=placed, out_specs=P("elem", "emit", None), check_vma=False
    )
```
